32 devices in a mesh: groups: 2 (over y), blocks: 4 (over z), halo: 2 (over x), gz: 2 (over core).
Axes of the slice: x: 2, y: 2, z: 4, core: 2. Of those that a mesh axis runs over, the one named last changes fastest.
Arguments:
- raw_volume: bfloat16 [256, 16, 128], P(('groups', 'blocks', 'gz'), 'halo'), parts along dimension 0, may hold values from -6 to 6
- tissue_counts: int32 [16, 2, 4], P(('groups', 'blocks', 'gz'), 'halo'), parts along dimension 0, may hold values from 0 to 8192, as said below
- patch_core_offsets: int32 [16, 2, 4], P(('groups', 'blocks', 'gz'), 'halo'), parts along dimension 0, may hold values from 0 to 8
- w_first: bfloat16 [64, 1, 3, 3, 3], replicated, may hold values from -1.25 to 1.25
- w_second: bfloat16 [27, 4096], replicated, may hold values from -0.15625 to 0.15625
- w_coarse: bfloat16 [27, 4096], replicated, may hold values from -0.15625 to 0.15625
- w_head: bfloat16 [3, 64], replicated, may hold values from -0.75 to 0.75
Outputs:
- affinities: float32 [3, 256, 16, 128], P(None, ('groups', 'blocks', 'gz'), 'halo'), parts along dimension 1
The draws below stay inside these ranges and needn't reach their ends.
There are 2 independent parts, one for each index of `groups`. The reference program is written for one: setup_inputs(seed, part) draws one part's arguments, and reference() takes and returns one part's arrays. A program takes and returns all parts, laid end to end along the dimension named above; an argument that names none is the same for every part. Nothing has to cross between parts.
Inputs may be any that keep to these rules, and one draw needn't show every extreme that they name: `tissue_counts`: in every group of 4 tiles that share their index along gz and their index h, exactly 4 slots are dense; a tile has at most 3 dense slots, and some tile of every such group has exactly 3.
All inputs are finite; a program needn't handle non-finite values.
Results may differ from the reference program's by a relative error of at most 0.004.
Values may be sent and summed in bfloat16 or wider, within the bound.
No kernel may reach another device: no remote copies, remote signals or barrier semaphores. Data moves between devices by JAX's collectives and lax.ppermute only.
A program may use at most 64 MiB of HBM per device.

```python
import jax
import jax.numpy as jnp
from jax import lax

C = 64
OUTC = 3
X = 128
TILE_VOXEL_DEPTH = 16
SY = 8
PATCH_CORE_DEPTH = 8
PATCH_SLOT_COUNT = 4
WORK = 1
MOST = 3
MINC = 4096
DEPTH_TILE_COUNT = 8
NZ = 128
NY = 16
N_BLOCKS = 4
N_HALO = 2
N_GZ = 2


def draw_tissue_counts(key, part):
    key = jax.random.fold_in(key, 11)
    key_blocks, key_slot_list, key_high, key_low = jax.random.split(key, 4)
    block_scores = jax.random.randint(key_blocks, (N_GZ, N_HALO, N_BLOCKS), 0, 1 << 20) * N_BLOCKS + jnp.arange(N_BLOCKS)
    block_pos = jnp.argsort(jnp.argsort(block_scores, axis=-1), axis=-1)
    profile = jnp.array([MOST, 1, 0, 0], jnp.int32)
    dense_count = profile[block_pos % 4]
    slot_ranking_values = jax.random.randint(key_slot_list, (N_GZ, N_HALO, N_BLOCKS, PATCH_SLOT_COUNT), 0, 1 << 20) * PATCH_SLOT_COUNT + jnp.arange(PATCH_SLOT_COUNT)
    slot_pos = jnp.argsort(jnp.argsort(slot_ranking_values, axis=-1), axis=-1)
    dense = slot_pos < dense_count[..., None]
    array_extent = (N_GZ, N_HALO, N_BLOCKS, PATCH_SLOT_COUNT)
    high = jax.random.randint(key_high, array_extent, MINC, PATCH_CORE_DEPTH * SY * X + 1)
    low = jax.random.randint(key_low, array_extent, 0, MINC)
    count_table = jnp.where(dense, high, low).astype(jnp.int32)
    count_table = jnp.transpose(count_table, (2, 0, 1, 3))
    return count_table.reshape(N_BLOCKS * N_GZ, N_HALO, PATCH_SLOT_COUNT)


def with_ends(drawn, rng, least, top_value):
    index_at = [jax.random.randint(jax.random.fold_in(rng, axis), (), 0, length) for axis, length in enumerate(drawn.shape)]
    widest = drawn.shape.index(max(drawn.shape))
    neighbour = index_at[:widest] + [(index_at[widest] + 1) % drawn.shape[widest]] + index_at[widest + 1:]
    return drawn.at[tuple(index_at)].set(least).at[tuple(neighbour)].set(top_value)


def levels(key, dims, pieces, least, largest):
    gain, own = 1.0, jax.random.fold_in(key, 6)
    for position, blocks in pieces:
        draws = jnp.exp(jax.random.uniform(jax.random.fold_in(own, position), (blocks,), jnp.float32, least / len(pieces), largest / len(pieces)))
        gain = gain * jnp.repeat(draws, dims[position] // blocks).reshape([-1 if axis == position else 1 for axis in range(len(dims))])
    return gain


def centred(stream_key, shape, spread, most, cuts=(), kind=jnp.bfloat16):
    drawn = spread * jax.random.normal(stream_key, shape, jnp.float32)
    if cuts:
        drawn = drawn * levels(stream_key, shape, cuts, -0.22, 0.18)
    return jnp.clip(drawn, -most, most).astype(kind)


def setup_inputs(seed: int = 0, part: int = 0) -> dict:
    keys = jax.random.split(jax.random.key(seed), 8)
    part_splits = jax.random.split(jax.random.fold_in(keys[7], part), 8)
    return {
        "raw_volume": centred(part_splits[0], (NZ, NY, X), 1.0, 6.0, ((0, 8), (1, 2))),
        "tissue_counts": draw_tissue_counts(jax.random.fold_in(jax.random.fold_in(keys[7], part), 71), part),
        "patch_core_offsets": with_ends(jax.random.randint(part_splits[2], (DEPTH_TILE_COUNT, N_HALO, PATCH_SLOT_COUNT), 0, TILE_VOXEL_DEPTH - PATCH_CORE_DEPTH + 1), jax.random.fold_in(part_splits[2], 1), 0, TILE_VOXEL_DEPTH - PATCH_CORE_DEPTH).astype(jnp.int32),
        "w_first": centred(keys[3], (C, 1, 3, 3, 3), 27 ** -0.5, 1.25),
        "w_second": centred(keys[4], (27, C * C), (27 * C) ** -0.5, 0.15625),
        "w_coarse": centred(keys[5], (27, C * C), (27 * C) ** -0.5, 0.15625),
        "w_head": centred(keys[6], (OUTC, C), C ** -0.5, 0.75),
    }


conv_dims = ("NCDHW", "OIDHW", "NCDHW")


def as_kernel(flat_weight):
    channels = w_channels(flat_weight)
    return jnp.transpose(flat_weight.reshape(3, 3, 3, channels, channels), (3, 4, 0, 1, 2))


def w_channels(flat_weight):
    total = flat_weight.shape[1]
    side = 1
    while side * side < total:
        side = side * 2
    return side


def convolve(inputs, kernel):
    result = lax.conv_general_dilated(inputs, kernel, (1, 1, 1), ((0, 0), (0, 0), (1, 1)), dimension_numbers=conv_dims, preferred_element_type=jnp.float32)
    return jnp.maximum(result, 0.0).astype(jnp.bfloat16)


def unet_level(window, w_first, w_second, w_coarse, w_head):
    batched = window[None, None]
    first_act = convolve(batched, w_first)
    second_act = convolve(first_act, as_kernel(w_second))
    depth, rows, cells = second_act.shape[2], second_act.shape[3], second_act.shape[4]
    pooled = second_act.astype(jnp.float32).reshape(1, C, depth // 2, 2, rows // 2, 2, cells // 2, 2)
    pooled = jnp.mean(pooled, axis=(3, 5, 7)).astype(jnp.bfloat16)
    coarse = convolve(pooled, as_kernel(w_coarse))
    upsampled = jnp.repeat(jnp.repeat(jnp.repeat(coarse, 2, axis=2), 2, axis=3), 2, axis=4)
    cropped = second_act[:, :, 2:depth - 2, 2:rows - 2, :]
    merged = (upsampled.astype(jnp.float32) + cropped.astype(jnp.float32)).astype(jnp.bfloat16)
    logits = jnp.einsum("oc,czyx->ozyx", w_head.astype(jnp.float32), merged[0].astype(jnp.float32))
    return jax.nn.sigmoid(logits).astype(jnp.bfloat16)


def reference(raw_volume, tissue_counts, patch_core_offsets, w_first, w_second, w_coarse, w_head):
    padded = jnp.pad(raw_volume, ((4, 4), (4, 4), (0, 0)))
    dense = (tissue_counts >= MINC).astype(jnp.int32).reshape(-1)
    active_total = N_BLOCKS * N_GZ * N_HALO * WORK
    active_sorting = jnp.argsort(1 - dense, stable=True)[:active_total].astype(jnp.int32)
    tile_position_index = active_sorting // (N_HALO * PATCH_SLOT_COUNT)
    margin_index = (active_sorting // PATCH_SLOT_COUNT) % N_HALO
    anchor_list = patch_core_offsets.reshape(-1)[active_sorting].astype(jnp.int32)
    z_starts = (tile_position_index * TILE_VOXEL_DEPTH + anchor_list).astype(jnp.int32)
    y_starts = (margin_index * SY).astype(jnp.int32)
    depth_pos = jnp.arange(PATCH_CORE_DEPTH).astype(jnp.float32)
    blend_weight = (depth_pos + 1.0) * (PATCH_CORE_DEPTH - depth_pos)
    blend_weight = blend_weight / jnp.max(blend_weight)
    zero_index = jnp.int32(0)

    def accumulate(totals, start_pair):
        numerator, coverage = totals
        z_start, y_start = start_pair
        window = lax.dynamic_slice(padded, (z_start, y_start, zero_index), (PATCH_CORE_DEPTH + 8, SY + 8, X))
        predicted = unet_level(window, w_first, w_second, w_coarse, w_head)
        weighted = predicted.astype(jnp.float32) * blend_weight[None, :, None, None]
        current = lax.dynamic_slice(numerator, (zero_index, z_start, y_start, zero_index), (OUTC, PATCH_CORE_DEPTH, SY, X))
        numerator = lax.dynamic_update_slice(numerator, current + weighted, (zero_index, z_start, y_start, zero_index))
        covered = lax.dynamic_slice(coverage, (z_start, y_start), (PATCH_CORE_DEPTH, SY))
        coverage = lax.dynamic_update_slice(coverage, covered + blend_weight[:, None], (z_start, y_start))
        return (numerator, coverage), None

    start_numer = jnp.zeros((OUTC, NZ, NY, X), jnp.float32)
    start_cover = jnp.zeros((NZ, NY), jnp.float32)
    (numerator, coverage), unused = lax.scan(accumulate, (start_numer, start_cover), (z_starts, y_starts))
    return numerator / jnp.maximum(coverage, 1.0)[None, :, :, None]
```

```python
import jax
import jax.numpy as jnp
from jax import lax
from jax.experimental import pallas as pl
from jax.experimental.pallas import tpu as pltpu
from jax.sharding import PartitionSpec as P

CORE = 8
MARGIN = 4
MOST = 3
MINC = 4096
F32 = jnp.float32
BF16 = jnp.bfloat16


def dot(a, b):
    return lax.dot_general(a, b, (((1,), (0,)), ((), ())), preferred_element_type=F32)


def dot_t(a, b):
    return lax.dot_general(a, b, (((1,), (1,)), ((), ())), preferred_element_type=F32)


def iota(shape, dim):
    return lax.broadcasted_iota(jnp.int32, shape, dim)


def tap_rows(flat_ref, rows_ref):
    taps = flat_ref.shape[0]
    for j in range(32):
        block = flat_ref[:, 128 * j : 128 * (j + 1)].astype(F32)
        rows_ref[pl.ds(2 * j, taps, stride=64), :] = block
        rows_ref[pl.ds(2 * j + 1, taps, stride=64), :] = pltpu.roll(block, 64, 1)


def band(rows_ref, taps):
    lower = iota((64, 128), 1) < 64
    w0, w1, w2 = (rows_ref[64 * t : 64 * (t + 1), :] for t in taps)
    d1 = jnp.concatenate([w1, w0], axis=0).T[:64]
    d2 = jnp.concatenate([w2, w1], axis=0).T[:64]
    d0 = jnp.where(lower, pltpu.roll(d1, 64, 1), 0.0)
    d3 = jnp.where(lower, 0.0, pltpu.roll(d2, 64, 1))
    return [d.astype(BF16) for d in (d0, d1, d2, d3)]


def prepare(first_ref, second_ref, coarse_ref, head_ref, w1_ref, w2_ref, wc_ref, wh_ref, rows_ref):
    shape = (256, 27)
    row, lane = iota(shape, 0), iota(shape, 1)
    xo, dz, y = row // 64, (row // 16) % 4, row % 16
    first = first_ref[...]
    parts = []
    for yy in range(2):
        for xx in range(2):
            dy, dx = y - yy, xo - xx
            valid = (dz < 3) & (dy >= 0) & (dy < 3) & (dx >= 0) & (dx < 3)
            pick = jnp.where(valid & (lane == dz * 9 + dy * 3 + dx), 1.0, 0.0).astype(BF16)
            parts.append(dot_t(pick, first))
    base = jnp.concatenate(parts, axis=1)
    for yp in range(7):
        moved = base if yp == 0 else pltpu.roll(base, 2 * yp, 0)
        w1_ref[:, 256 * yp : 256 * (yp + 1)] = moved.astype(BF16)

    tap_rows(second_ref, rows_ref)
    zeros = jnp.zeros((256, 128), BF16)
    for dz in range(3):
        for dy in range(3):
            blocks = band(rows_ref, [9 * dz + 3 * dy + dx for dx in range(3)])
            for yy in range(2):
                for xi in range(4):
                    at = 256 * (4 * dz + dy + yy) + 64 * xi
                    w2_ref[at : at + 64, 128 * yy : 128 * (yy + 1)] = blocks[xi]
        w2_ref[1024 * dz : 1024 * dz + 256, 128:256] = zeros
        w2_ref[1024 * dz + 768 : 1024 * dz + 1024, 0:128] = zeros

    tap_rows(coarse_ref, rows_ref)
    zeros = jnp.zeros((128, 128), BF16)
    for dz in range(3):
        for dx in range(3):
            blocks = band(rows_ref, [9 * dz + 3 * dy + dx for dy in range(3)])
            start = 384 * (3 * dz + dx)
            for half in range(2):
                for d in range(4):
                    at = start + 64 * (d + 2 * half)
                    wc_ref[at : at + 64, 128 * half : 128 * (half + 1)] = blocks[d]
            wc_ref[start + 256 : start + 384, 0:128] = zeros
            wc_ref[start : start + 128, 128:256] = zeros

    wide = (192, 256)
    row, lane = iota(wide, 0), iota(wide, 1)
    yp, xx, y = row // 48, (row // 24) % 2, row % 8
    o = (row // 8) % 3
    head = head_ref[...].astype(F32)
    tiled = jnp.concatenate([head] * 4, axis=1)
    value = jnp.where(o == 0, tiled[0:1], jnp.where(o == 1, tiled[1:2], tiled[2:3]))
    valid = (y // 2 == yp) & (y % 2 == lane // 128) & (xx == (lane // 64) % 2)
    wh_ref[...] = jnp.where(valid, value, 0.0).astype(BF16)


def tile_kernel(
    halo_count,
    tile_count,
    counts_ref,
    offsets_ref,
    raw_ref,
    *refs,
):
    ysides = refs[: 1 + (halo_count > 2)]
    refs = refs[len(ysides) :]
    (pair_ref, chain_ref, w1_ref, w2_ref, wc_ref, wh_ref, out_ref) = refs[:7]
    (ext_ref, a_ref, s_ref, q_ref, lc_ref, cr_ref, num_ref) = refs[7:]

    halo_index = lax.axis_index("halo")
    gz_index = lax.axis_index("gz")
    tile_index = lax.axis_index("blocks") * 2 + gz_index

    slots = counts_ref.shape[2]
    dense = [(counts_ref[0, 0, s] >= MINC).astype(jnp.int32) for s in range(slots)]
    total = jnp.int32(0)
    anchors = [jnp.int32(0)] * MOST
    for s in range(slots):
        for j in range(MOST):
            anchors[j] = anchors[j] + jnp.where(total == j, dense[s], 0) * offsets_ref[0, 0, s]
        total = total + dense[s]
    anchors = [jnp.where(j < total, anchors[j], anchors[0]) for j in range(MOST)]
    low = jnp.minimum(jnp.minimum(anchors[0], anchors[1]), anchors[2])
    high = jnp.maximum(jnp.maximum(anchors[0], anchors[1]), anchors[2])
    pairs = (high - low + 13) // 2
    start = jnp.minimum(low, 20 - 2 * pairs)

    @pl.when(total == 0)
    def _():
        out_ref[...] = jnp.zeros_like(out_ref)

    @pl.when(total > 0)
    def _():
        odd_h = halo_index % 2 == 1
        odd_g = gz_index == 1

        def with_rows(own, sides):
            own = own.astype(F32)
            near = sides[0].astype(F32)
            far = sides[1].astype(F32) if len(sides) > 1 else jnp.zeros_like(near)
            below = jnp.where(odd_h, near, far)
            above = jnp.where(odd_h, far, near)
            return jnp.concatenate([below[:, 4:8], own, above[:, 0:4]], axis=1)

        core = with_rows(raw_ref[...], [r[...] for r in ysides])
        pair = with_rows(pair_ref[0], [pair_ref[1 + k] for k in range(len(ysides))])
        chain = with_rows(chain_ref[0], [chain_ref[1 + k] for k in range(len(ysides))])
        edge = jnp.where(odd_g, tile_index == tile_count - 1, tile_index == 0)
        chain = jnp.where(edge, 0.0, chain)
        below = jnp.where(odd_g, pair, chain)
        above = jnp.where(odd_g, chain, pair)
        ext = jnp.concatenate([below, core, above, jnp.zeros((2, 16, 128), F32)], axis=0)
        ext = ext.reshape(26 * 16, 128)
        moved = jnp.where(iota(ext.shape, 1) < 127, pltpu.roll(ext, 127, 1), 0.0)
        ext_ref[0] = ext.astype(BF16).reshape(26, 16, 128)
        ext_ref[1] = moved.astype(BF16).reshape(26, 16, 128)

        row, lane = iota((192, 128), 0), iota((192, 128), 1)
        select = jnp.where(lane == 2 * (row % 64) - 2 + 2 * (row // 64), 1.0, 0.0).astype(BF16)
        edge_rows, edge_lanes = iota((16, 128), 0), iota((16, 128), 1)
        keep_first = (edge_rows > 0) | (edge_lanes >= 64)
        keep_last = (edge_rows < 15) | (edge_lanes < 64)

        def first_step(k, carry):
            z = start + 2 * k
            around = jnp.concatenate(
                [ext_ref[m, pl.ds(z + d, 4)].reshape(64, 128) for d in range(2) for m in range(2)],
                axis=0,
            )
            u = dot_t(select, around).astype(BF16)
            rows = []
            for d in range(2):
                tiles = [u[64 * m : 64 * (m + 1), 128 * d : 128 * (d + 1)] for m in range(3)]
                rows.append(jnp.concatenate(tiles[:2], axis=1))
                rows.append(jnp.concatenate(tiles[1:], axis=1))
            lhs = jnp.concatenate(rows, axis=0)
            for yp in range(7):
                res = jnp.maximum(dot(lhs, w1_ref[:, 256 * yp : 256 * (yp + 1)]), 0.0)
                for d in range(2):
                    for half in range(2):
                        at = 64 * (2 * d + half)
                        for yy in range(2):
                            tile = res[at : at + 64, 128 * yy : 128 * (yy + 1)]
                            if half == 0:
                                head = jnp.where(keep_first, tile[:16], 0.0)
                                tile = jnp.concatenate([head, tile[16:]], axis=0)
                            else:
                                tail = jnp.where(keep_last, tile[48:], 0.0)
                                tile = jnp.concatenate([tile[:48], tail], axis=0)
                            a_ref[z + d, yy, yp, :, 128 * half : 128 * (half + 1)] = tile.astype(BF16)
            return carry

        lax.fori_loop(0, pairs + 1, first_step, 0)

        lower_half = iota((64, 128), 1) < 64

        def second_step(k, carry):
            z = start + 2 * k
            total_sum = None
            for dz in range(3):
                for y in range(4):
                    lhs = a_ref[pl.ds(z + dz, 2), y % 2, pl.ds(y // 2, 6)].reshape(768, 256)
                    at = 256 * (4 * dz + y)
                    term = dot(lhs, w2_ref[at : at + 256, :])
                    total_sum = term if total_sum is None else total_sum + term
            act = jnp.maximum(total_sum, 0.0).astype(BF16)
            s_ref[pl.ds(z, 2)] = act.reshape(2, 6, 64, 256)
            full = act.astype(F32)
            both = full[:, :128] + full[:, 128:]
            both = both + pltpu.roll(both, 64, 1)
            both = both.reshape(2, 6, 64, 128)
            for d in range(2):
                for j in range(3):
                    q_ref[z + d, j] = jnp.where(lower_half, both[d, 2 * j], both[d, 2 * j + 1])
            return carry

        lax.fori_loop(0, pairs, second_step, 0)

        rows64 = iota((64, 128), 0)
        for j in range(MOST):
            for k in range(6):
                for m in range(3):
                    z = anchors[j] + 2 * k
                    mean = (q_ref[z, m] + q_ref[z + 1, m]) * 0.125
                    before = jnp.where(rows64 == 0, 0.0, pltpu.roll(mean, 1, 0))
                    after = jnp.where(rows64 == 63, 0.0, pltpu.roll(mean, 63, 0))
                    for dx, value in enumerate((before, mean, after)):
                        at = 384 * dx + 128 * m
                        lc_ref[j, k, :, at : at + 128] = value.astype(BF16)

        coarse = None
        for dz in range(3):
            lhs = lc_ref[:, dz : dz + 4].reshape(MOST * 256, 1152)
            term = dot(lhs, wc_ref[1152 * dz : 1152 * (dz + 1), :])
            coarse = term if coarse is None else coarse + term
        coarse = jnp.maximum(coarse, 0.0).astype(BF16).astype(F32)
        coarse = coarse.reshape(MOST, 4, 64, 256)
        for j in range(MOST):
            for k in range(4):
                for m in range(2):
                    tile = coarse[j, k, :, 128 * m : 128 * (m + 1)]
                    turned = pltpu.roll(tile, 64, 1)
                    cr_ref[j, k, 2 * m] = jnp.where(lower_half, tile, turned)
                    cr_ref[j, k, 2 * m + 1] = jnp.where(lower_half, turned, tile)

        num_ref[...] = jnp.zeros_like(num_ref)
        lower24 = iota((24, 128), 1) < 64
        row, lane = iota((128, 128), 0), iota((128, 128), 1)
        order = jnp.where(lane == 2 * (row % 64) + row // 64, 1.0, 0.0).astype(BF16)
        for j in range(MOST):
            present = (j < total).astype(F32)
            for group in range(2):
                logits = None
                for yp in range(4):
                    planes = []
                    for u in range(4):
                        depth = 4 * group + u
                        fine = s_ref[anchors[j] + 2 + depth, yp + 1].astype(F32)
                        up = cr_ref[j, depth // 2, yp]
                        planes.append(fine + jnp.concatenate([up, up], axis=1))
                    merged = jnp.concatenate(planes, axis=0).astype(BF16)
                    term = dot_t(wh_ref[48 * yp : 48 * (yp + 1), :], merged)
                    logits = term if logits is None else logits + term
                pred = jax.nn.sigmoid(logits).astype(BF16).astype(F32)
                lhs = []
                for u in range(4):
                    tile = pred[:, 128 * (u // 2) : 128 * (u // 2 + 1)]
                    even, odd = tile[:24], tile[24:]
                    if u % 2 == 0:
                        lhs.append(jnp.where(lower24, even, pltpu.roll(odd, 64, 1)))
                    else:
                        lhs.append(jnp.where(lower24, pltpu.roll(even, 64, 1), odd))
                ordered = dot(jnp.concatenate(lhs, axis=0).astype(BF16), order)
                for u in range(4):
                    depth = 4 * group + u
                    weight = (depth + 1.0) * (CORE - depth) / 20.0
                    value = ordered[24 * u : 24 * (u + 1)].reshape(3, 8, 128)
                    at = anchors[j] + depth
                    num_ref[at] = num_ref[at] + value * (present * weight)
        for z in range(16):
            cover = jnp.float32(0.0)
            for j in range(MOST):
                u = z - anchors[j]
                uf = u.astype(F32)
                tent = (uf + 1.0) * (CORE - uf) * 0.05
                inside = (j < total) & (u >= 0) & (u < CORE)
                cover = cover + jnp.where(inside, tent, 0.0)
            below = jnp.maximum(jnp.full((8, 128), cover, F32), 1.0)
            for c in range(3):
                out_ref[c, z] = num_ref[z, c] / below


def neighbour_pairs(count, first, closed):
    pairs = []
    for i in range(first, count - 1, 2):
        pairs += [(i, i + 1), (i + 1, i)]
    if closed:
        pairs += [(0, count - 1), (count - 1, 0)]
    return pairs


def local(raw_volume, tissue_counts, patch_core_offsets, w_first, w_second, w_coarse, w_head):
    halo_count = lax.axis_size("halo")
    tile_count = lax.axis_size("blocks") * lax.axis_size("gz")
    vmem = pl.BlockSpec(memory_space=pltpu.VMEM)
    smem = pl.BlockSpec(memory_space=pltpu.SMEM)

    ysides = [lax.ppermute(raw_volume, "halo", neighbour_pairs(halo_count, 0, False))]
    if halo_count > 2:
        ysides.append(lax.ppermute(raw_volume, "halo", neighbour_pairs(halo_count, 1, False)))

    w1, w2, wc, wh = pl.pallas_call(
        prepare,
        out_shape=[
            jax.ShapeDtypeStruct((256, 1792), BF16),
            jax.ShapeDtypeStruct((3072, 256), BF16),
            jax.ShapeDtypeStruct((3456, 256), BF16),
            jax.ShapeDtypeStruct((192, 256), BF16),
        ],
        in_specs=[vmem] * 4,
        out_specs=[vmem] * 4,
        scratch_shapes=[pltpu.VMEM((27 * 64, 128), F32)],
        compiler_params=pltpu.CompilerParams(vmem_limit_bytes=24 << 20),
        cost_estimate=pl.CostEstimate(flops=1 << 20, bytes_accessed=8 << 20, transcendentals=0),
    )(w_first.reshape(64, 27), w_second, w_coarse, w_head)

    stack = jnp.stack([raw_volume] + ysides)
    odd = lax.axis_index("gz") == 1
    head, tail = stack[:, :MARGIN], stack[:, -MARGIN:]
    pair = lax.ppermute(jnp.where(odd, head, tail), "gz", [(0, 1), (1, 0)])
    chain = lax.ppermute(
        jnp.where(odd, tail, head), ("blocks", "gz"), neighbour_pairs(tile_count, 1, True)
    )

    def body(*refs):
        tile_kernel(halo_count, tile_count, *refs)

    return pl.pallas_call(
        body,
        out_shape=jax.ShapeDtypeStruct((3, 16, 8, 128), F32),
        in_specs=[smem, smem] + [vmem] * (7 + len(ysides)),
        out_specs=vmem,
        scratch_shapes=[
            pltpu.VMEM((2, 26, 16, 128), BF16),
            pltpu.VMEM((22, 2, 7, 64, 256), BF16),
            pltpu.VMEM((20, 6, 64, 256), BF16),
            pltpu.VMEM((20, 3, 64, 128), F32),
            pltpu.VMEM((MOST, 6, 64, 1152), BF16),
            pltpu.VMEM((MOST, 4, 4, 64, 128), F32),
            pltpu.VMEM((16, 3, 8, 128), F32),
        ],
        compiler_params=pltpu.CompilerParams(vmem_limit_bytes=48 << 20),
        cost_estimate=pl.CostEstimate(flops=20 << 30, bytes_accessed=5 << 20, transcendentals=0),
    )(tissue_counts, patch_core_offsets, raw_volume, *ysides, pair, chain, w1, w2, wc, wh)


def solution(mesh):
    in_specs = (
        P(("groups", "blocks", "gz"), "halo", None),
        P(("groups", "blocks", "gz"), "halo", None),
        P(("groups", "blocks", "gz"), "halo", None),
        P(),
        P(),
        P(),
        P(),
    )
    out_specs = P(None, ("groups", "blocks", "gz"), "halo", None)
    return jax.shard_map(local, mesh=mesh, in_specs=in_specs, out_specs=out_specs, check_vma=False)
```

```python
import jax
import jax.numpy as jnp
from jax import lax
from jax.experimental import pallas as pl
from jax.experimental.pallas import tpu as pltpu
from jax.sharding import PartitionSpec as P

CORE = 8
MARGIN = 4
MOST = 3
MINC = 4096
F32 = jnp.float32
BF16 = jnp.bfloat16
HBM = pltpu.HBM


def dot(a, b):
    return lax.dot_general(a, b, (((1,), (0,)), ((), ())), preferred_element_type=F32)


def dot_t(a, b):
    return lax.dot_general(a, b, (((1,), (1,)), ((), ())), preferred_element_type=F32)


def iota(shape, dim):
    return lax.broadcasted_iota(jnp.int32, shape, dim)


def tap_rows(flat_ref, rows_ref):
    taps = flat_ref.shape[0]
    for j in range(32):
        block = flat_ref[:, 128 * j : 128 * (j + 1)].astype(F32)
        rows_ref[pl.ds(2 * j, taps, stride=64), :] = block
        rows_ref[pl.ds(2 * j + 1, taps, stride=64), :] = pltpu.roll(block, 64, 1)


def band(w0, w1, w2):
    lower = iota((64, 128), 1) < 64
    d1 = jnp.concatenate([w1, w0], axis=0).T[:64]
    d2 = jnp.concatenate([w2, w1], axis=0).T[:64]
    d0 = jnp.where(lower, pltpu.roll(d1, 64, 1), 0.0)
    d3 = jnp.where(lower, 0.0, pltpu.roll(d2, 64, 1))
    return [d.astype(BF16) for d in (d0, d1, d2, d3)]


def put_bands(out_ref, start, blocks, columns):
    for i, block in enumerate(blocks):
        out_ref[start + 64 * i : start + 64 * (i + 1), columns : columns + 128] = block


def prepare_first(first_hbm, second_hbm, coarse_hbm, head_hbm, raw_hbm, *refs):
    (w1_ref, w2_ref, wh_ref, raw_ref, coarse_ref) = refs[:5]
    (rows_ref, first_ref, second_ref, head_ref, sems) = refs[5:]
    copies = [
        pltpu.make_async_copy(src, dst, sems.at[i])
        for i, (src, dst) in enumerate(
            (
                (second_hbm, second_ref),
                (first_hbm, first_ref),
                (head_hbm, head_ref),
                (raw_hbm, raw_ref),
                (coarse_hbm, coarse_ref),
            )
        )
    ]
    for copy in copies:
        copy.start()

    shape = (256, 27)
    row, lane = iota(shape, 0), iota(shape, 1)
    xo, dz, y = row // 64, (row // 16) % 4, row % 16
    picks = []
    for yy in range(2):
        for xx in range(2):
            dy, dx = y - yy, xo - xx
            valid = (dz < 3) & (dy >= 0) & (dy < 3) & (dx >= 0) & (dx < 3)
            picks.append(jnp.where(valid & (lane == dz * 9 + dy * 3 + dx), 1.0, 0.0).astype(BF16))
    for copy in copies[1:]:
        copy.wait()
    first = jnp.concatenate(
        [first_ref[0, k // 3, k % 3].astype(F32) for k in range(9)], axis=0
    ).astype(BF16)
    base = jnp.concatenate([dot(pick, first) for pick in picks], axis=1)
    for yp in range(7):
        moved = base if yp == 0 else pltpu.roll(base, 2 * yp, 0)
        w1_ref[:, 256 * yp : 256 * (yp + 1)] = moved.astype(BF16)

    wide = (240, 256)
    row, lane = iota(wide, 0), iota(wide, 1)
    yp, xx, y = row // 48, (row // 24) % 2, row % 8
    o = (row // 8) % 3
    head = head_ref[...].astype(F32)
    tiled = jnp.concatenate([head] * 4, axis=1)
    value = jnp.where(o == 0, tiled[0:1], jnp.where(o == 1, tiled[1:2], tiled[2:3]))
    fine = (y // 2 == yp) & (y % 2 == lane // 128) & (xx == (lane // 64) % 2)
    up = (yp == 4) & (y // 2 == lane // 64)
    wh_ref[...] = jnp.where(fine | up, value, 0.0).astype(BF16)

    copies[0].wait()
    tap_rows(second_ref, rows_ref)
    zeros = jnp.zeros((256, 128), BF16)
    for w in range(4):
        for dy in range(3):
            taps = []
            for dx in range(3):
                g0, g1, g2 = (
                    rows_ref[64 * t : 64 * (t + 1), :] for t in range(3 * dy + dx, 27, 9)
                )
                taps.append((g0, 0.5 * (g0 + g1 + g2), 0.5 * (g0 - g1 + g2), g2)[w])
            blocks = band(*taps)
            for yy in range(2):
                put_bands(w2_ref, 256 * (4 * w + dy + yy), blocks, 128 * yy)
        w2_ref[1024 * w : 1024 * w + 256, 128:256] = zeros
        w2_ref[1024 * w + 768 : 1024 * w + 1024, 0:128] = zeros


def prepare_coarse(coarse_ref, wc_ref, rows_ref):
    tap_rows(coarse_ref, rows_ref)
    zeros = jnp.zeros((128, 128), BF16)
    for dz in range(3):
        for dx in range(3):
            blocks = band(
                *(rows_ref[64 * t : 64 * (t + 1), :] for t in range(9 * dz + dx, 9 * dz + 9, 3))
            )
            start = 384 * (3 * dz + dx)
            for half in range(2):
                put_bands(wc_ref, start + 128 * half, blocks, 128 * half)
            wc_ref[start + 256 : start + 384, 0:128] = zeros
            wc_ref[start : start + 128, 128:256] = zeros


def side_by_side(logits):
    lower = iota((24, 128), 1) < 64
    planes = []
    for half in range(2):
        tile = logits[:, 128 * half : 128 * (half + 1)]
        even, odd = tile[:24], tile[24:]
        planes.append(jnp.where(lower, even, pltpu.roll(odd, 64, 1)))
        planes.append(jnp.where(lower, pltpu.roll(even, 64, 1), odd))
    return planes


def tile_kernel(halo_count, tile_count, counts_hbm, offsets_hbm, raw_ref, *refs):
    ysides = refs[: 1 + (halo_count > 2)]
    refs = refs[len(ysides) :]
    (pair_ref, chain_ref, w1_ref, w2_ref, wc_ref, wh_ref, out_ref) = refs[:7]
    (ext_ref, u_ref, a_ref, q_ref, lc_ref, fine_ref, up_ref, pred_ref) = refs[7:15]
    counts_ref, offsets_ref, sems = refs[15:]
    copies = [
        pltpu.make_async_copy(counts_hbm, counts_ref, sems.at[0]),
        pltpu.make_async_copy(offsets_hbm, offsets_ref, sems.at[1]),
    ]
    for copy in copies:
        copy.start()

    halo_index = lax.axis_index("halo")
    gz_index = lax.axis_index("gz")
    tile_index = lax.axis_index("blocks") * 2 + gz_index

    odd_h = halo_index % 2 == 1
    odd_g = gz_index == 1

    def with_rows(own, sides):
        own = own.astype(F32)
        near = sides[0].astype(F32)
        far = sides[1].astype(F32) if len(sides) > 1 else jnp.zeros_like(near)
        below = jnp.where(odd_h, near, far)
        above = jnp.where(odd_h, far, near)
        return jnp.concatenate([below[:, 4:8], own, above[:, 0:4]], axis=1)

    core = with_rows(raw_ref[...], [r[...] for r in ysides])
    pair = with_rows(pair_ref[0], [pair_ref[1 + k] for k in range(len(ysides))])
    chain = with_rows(chain_ref[0], [chain_ref[1 + k] for k in range(len(ysides))])
    edge = jnp.where(odd_g, tile_index == tile_count - 1, tile_index == 0)
    chain = jnp.where(edge, 0.0, chain)
    below = jnp.where(odd_g, pair, chain)
    above = jnp.where(odd_g, chain, pair)
    ext = jnp.concatenate([below, core, above, jnp.zeros((2, 16, 128), F32)], axis=0)
    ext = ext.reshape(26 * 16, 128)
    moved = jnp.where(iota(ext.shape, 1) < 127, pltpu.roll(ext, 127, 1), 0.0)
    ext_ref[0] = ext.astype(BF16).reshape(26, 16, 128)
    ext_ref[1] = moved.astype(BF16).reshape(26, 16, 128)

    row, lane = iota((160, 128), 0), iota((160, 128), 1)
    select = jnp.where(lane == 2 * (row % 80) - 2 + 2 * (row // 80), 1.0, 0.0).astype(BF16)
    for z in range(0, 22, 2):
        around = jnp.concatenate(
            [ext_ref[m, z + d : z + d + 4].reshape(64, 128) for d in range(2) for m in range(2)],
            axis=0,
        )
        u = dot_t(select, around).astype(BF16)
        for d in range(2):
            for m in range(2):
                u_ref[z + d, :, 128 * m : 128 * (m + 1)] = u[
                    80 * m : 80 * (m + 1), 128 * d : 128 * (d + 1)
                ]

    edge_rows, edge_lanes = iota((8, 128), 0), iota((8, 128), 1)
    keep_first = (edge_rows > 0) | (edge_lanes >= 64)
    keep_last = (edge_rows < 1) & (edge_lanes < 64)

    def first_step(k, carry):
        z = 11 * k
        lhs = u_ref[pl.ds(z, 11)].reshape(880, 256)
        for yp in range(7):
            res = jnp.maximum(dot(lhs, w1_ref[:, 256 * yp : 256 * (yp + 1)]), 0.0)
            for d in range(11):
                for yy in range(2):
                    tile = res[80 * d : 80 * d + 72, 128 * yy : 128 * (yy + 1)]
                    head = jnp.where(keep_first, tile[:8], 0.0)
                    tail = jnp.where(keep_last, tile[64:], 0.0)
                    tile = jnp.concatenate([head, tile[8:64], tail], axis=0)
                    a_ref[z + d, yy, yp, :, 0:128] = tile[:64].astype(BF16)
                    after = pltpu.roll(tile, 71, 0)[:64]
                    a_ref[z + d, yy, yp, :, 128:256] = after.astype(BF16)
        return carry

    lax.fori_loop(0, 2, first_step, 0)

    lower_half = iota((64, 128), 1) < 64

    def second_step(k, carry):
        z = 4 * k
        products = []
        for w, (i, j) in enumerate(((0, 2), (1, 2), (2, 1), (1, 3))):
            mixed = []
            for p in range(2):
                first, second = a_ref[z + 2 * p + i], a_ref[z + 2 * p + j]
                mixed.append(first + second if w == 1 else first - second)
            product = None
            for y in range(4):
                lhs = jnp.concatenate(
                    [m[y % 2, y // 2 : y // 2 + 6].reshape(384, 256) for m in mixed], axis=0
                )
                at = 256 * (4 * w + y)
                term = dot(lhs, w2_ref[at : at + 256, :])
                product = term if product is None else product + term
            products.append(product)
        m0, m1, m2, m3 = products
        acts = [m0 + m1 + m2, m1 - m2 - m3]
        acts = [jnp.maximum(act, 0.0).astype(BF16).reshape(2, 6, 64, 256) for act in acts]
        planes = [acts[d % 2][d // 2] for d in range(4)]
        logits = None
        for yp in range(4):
            rows = jnp.concatenate([plane[yp + 1] for plane in planes], axis=0)
            term = dot_t(wh_ref[48 * yp : 48 * (yp + 1), :], rows)
            logits = term if logits is None else logits + term
        for d, plane in enumerate(side_by_side(logits)):
            fine_ref[z + d] = plane
        for d, plane in enumerate(planes):
            full = plane.astype(F32)
            both = full[:, :, :128] + full[:, :, 128:]
            for j in range(3):
                even, odd = both[2 * j], both[2 * j + 1]
                even = even + pltpu.roll(even, 64, 1)
                odd = odd + pltpu.roll(odd, 64, 1)
                q_ref[z + d, j] = jnp.where(lower_half, even, odd)
        return carry

    lax.fori_loop(0, 5, second_step, 0)

    for copy in copies:
        copy.wait()
    slots = counts_ref.shape[2]
    total = jnp.int32(0)
    anchors = [jnp.int32(0)] * MOST
    for s in range(slots):
        dense = counts_ref[0, 0, s] >= MINC
        for j in range(MOST):
            anchors[j] = jnp.where(dense & (total == j), offsets_ref[0, 0, s], anchors[j])
        total = total + dense.astype(jnp.int32)

    rows64 = iota((64, 128), 0)
    for j in range(MOST):
        for k in range(6):
            for m in range(3):
                z = anchors[j] + 2 * k
                mean = (q_ref[z, m] + q_ref[z + 1, m]) * 0.125
                before = jnp.where(rows64 == 0, 0.0, pltpu.roll(mean, 1, 0))
                after = jnp.where(rows64 == 63, 0.0, pltpu.roll(mean, 63, 0))
                for dx, value in enumerate((before, mean, after)):
                    at = 384 * dx + 128 * m
                    lc_ref[j, k, :, at : at + 128] = value.astype(BF16)

    coarse = None
    for dz in range(3):
        lhs = lc_ref[:, dz : dz + 4].reshape(MOST * 256, 1152)
        term = dot(lhs, wc_ref[1152 * dz : 1152 * (dz + 1), :])
        coarse = term if coarse is None else coarse + term
    coarse = jnp.maximum(coarse, 0.0).astype(BF16)
    for j in range(MOST):
        logits = dot_t(wh_ref[192:240, :], coarse[256 * j : 256 * (j + 1)])
        for k, plane in enumerate(side_by_side(logits)):
            up_ref[j, k] = plane

    row, lane = iota((128, 128), 0), iota((128, 128), 1)
    order = jnp.where(lane == 2 * (row % 64) + row // 64, 1.0, 0.0).astype(BF16)
    preds = []
    for j in range(MOST):
        for u in range(CORE):
            logits = fine_ref[anchors[j] + 2 + u] + up_ref[j, u // 2]
            preds.append(jax.nn.sigmoid(logits))
    ordered = dot(jnp.concatenate(preds, axis=0).astype(BF16), order)
    pred_ref[...] = ordered.reshape(MOST, CORE, 3, 8, 128)

    for z in range(16):
        cover = jnp.float32(0.0)
        value = jnp.zeros((3, 8, 128), F32)
        for j in range(MOST):
            u = z - anchors[j]
            uf = u.astype(F32)
            tent = (uf + 1.0) * (CORE - uf) / 20.0
            inside = (j < total) & (u >= 0) & (u < CORE)
            tent = jnp.where(inside, tent, 0.0)
            cover = cover + tent
            value = value + pred_ref[j, jnp.clip(u, 0, CORE - 1)] * tent
        value = value / jnp.maximum(jnp.full((8, 128), cover, F32), 1.0)
        for c in range(3):
            out_ref[c, z] = value[c]


def neighbour_pairs(count, first, closed):
    pairs = []
    for i in range(first, count - 1, 2):
        pairs += [(i, i + 1), (i + 1, i)]
    if closed:
        pairs += [(0, count - 1), (count - 1, 0)]
    return pairs


def local(raw_volume, tissue_counts, patch_core_offsets, w_first, w_second, w_coarse, w_head):
    halo_count = lax.axis_size("halo")
    tile_count = lax.axis_size("blocks") * lax.axis_size("gz")
    vmem = pl.BlockSpec(memory_space=pltpu.VMEM)
    hbm = pl.BlockSpec(memory_space=HBM)

    ysides = [lax.ppermute(raw_volume, "halo", neighbour_pairs(halo_count, 0, False))]
    if halo_count > 2:
        ysides.append(lax.ppermute(raw_volume, "halo", neighbour_pairs(halo_count, 1, False)))

    first_taps = jnp.transpose(w_first, (1, 2, 3, 4, 0))
    w1, w2, wh, raw, coarse = pl.pallas_call(
        prepare_first,
        out_shape=[
            jax.ShapeDtypeStruct((256, 1792), BF16),
            jax.ShapeDtypeStruct((4096, 256), BF16),
            jax.ShapeDtypeStruct((240, 256), BF16),
            jax.ShapeDtypeStruct(raw_volume.shape, BF16),
            jax.ShapeDtypeStruct(w_coarse.shape, BF16),
        ],
        in_specs=[hbm] * 5,
        out_specs=[vmem] * 5,
        scratch_shapes=[
            pltpu.VMEM((27 * 64, 128), F32),
            pltpu.VMEM(first_taps.shape, BF16),
            pltpu.VMEM(w_second.shape, BF16),
            pltpu.VMEM(w_head.shape, BF16),
            pltpu.SemaphoreType.DMA((5,)),
        ],
        compiler_params=pltpu.CompilerParams(vmem_limit_bytes=24 << 20),
        cost_estimate=pl.CostEstimate(flops=1 << 20, bytes_accessed=8 << 20, transcendentals=0),
    )(first_taps, w_second, w_coarse, w_head, raw_volume)

    stack = jnp.stack([raw] + ysides)
    odd = lax.axis_index("gz") == 1
    head, tail = stack[:, :MARGIN], stack[:, -MARGIN:]
    pair = lax.ppermute(jnp.where(odd, head, tail), "gz", [(0, 1), (1, 0)])
    chain = lax.ppermute(
        jnp.where(odd, tail, head), ("blocks", "gz"), neighbour_pairs(tile_count, 1, True)
    )

    wc = pl.pallas_call(
        prepare_coarse,
        out_shape=jax.ShapeDtypeStruct((3456, 256), BF16),
        in_specs=[vmem],
        out_specs=vmem,
        scratch_shapes=[pltpu.VMEM((27 * 64, 128), F32)],
        compiler_params=pltpu.CompilerParams(vmem_limit_bytes=16 << 20),
        cost_estimate=pl.CostEstimate(flops=1 << 20, bytes_accessed=6 << 20, transcendentals=0),
    )(coarse)

    def body(*refs):
        tile_kernel(halo_count, tile_count, *refs)

    return pl.pallas_call(
        body,
        out_shape=jax.ShapeDtypeStruct((3, 16, 8, 128), F32),
        in_specs=[hbm, hbm] + [vmem] * (7 + len(ysides)),
        out_specs=vmem,
        scratch_shapes=[
            pltpu.VMEM((2, 26, 16, 128), BF16),
            pltpu.VMEM((22, 80, 256), BF16),
            pltpu.VMEM((22, 2, 7, 64, 256), BF16),
            pltpu.VMEM((20, 3, 64, 128), F32),
            pltpu.VMEM((MOST, 6, 64, 1152), BF16),
            pltpu.VMEM((20, 24, 128), F32),
            pltpu.VMEM((MOST, 4, 24, 128), F32),
            pltpu.VMEM((MOST, CORE, 3, 8, 128), F32),
            pltpu.SMEM(tissue_counts.shape, jnp.int32),
            pltpu.SMEM(patch_core_offsets.shape, jnp.int32),
            pltpu.SemaphoreType.DMA((2,)),
        ],
        compiler_params=pltpu.CompilerParams(vmem_limit_bytes=40 << 20),
        cost_estimate=pl.CostEstimate(flops=16 << 30, bytes_accessed=5 << 20, transcendentals=0),
    )(tissue_counts, patch_core_offsets, raw, *ysides, pair, chain, w1, w2, wc, wh)


def solution(mesh):
    in_specs = (
        P(("groups", "blocks", "gz"), "halo", None),
        P(("groups", "blocks", "gz"), "halo", None),
        P(("groups", "blocks", "gz"), "halo", None),
        P(),
        P(),
        P(),
        P(),
    )
    out_specs = P(None, ("groups", "blocks", "gz"), "halo", None)
    return jax.shard_map(local, mesh=mesh, in_specs=in_specs, out_specs=out_specs, check_vma=False)
```

```python
import jax
import jax.numpy as jnp
from jax import lax
from jax.experimental import pallas as pl
from jax.experimental.pallas import tpu as pltpu
from jax.sharding import PartitionSpec as P

CORE = 8
MARGIN = 4
MOST = 3
MINC = 4096
F32 = jnp.float32
BF16 = jnp.bfloat16
HBM = pltpu.HBM


def dot(a, b):
    return lax.dot_general(a, b, (((1,), (0,)), ((), ())), preferred_element_type=F32)


def dot_t(a, b):
    return lax.dot_general(a, b, (((1,), (1,)), ((), ())), preferred_element_type=F32)


def iota(shape, dim):
    return lax.broadcasted_iota(jnp.int32, shape, dim)


def tap_rows(flat_ref, rows_ref):
    taps = flat_ref.shape[0]
    for j in range(32):
        block = flat_ref[:, 128 * j : 128 * (j + 1)].astype(F32)
        rows_ref[pl.ds(2 * j, taps, stride=64), :] = block
        rows_ref[pl.ds(2 * j + 1, taps, stride=64), :] = pltpu.roll(block, 64, 1)


def band(w0, w1, w2):
    lower = iota((64, 128), 1) < 64
    d1 = jnp.concatenate([w1, w0], axis=0).T[:64]
    d2 = jnp.concatenate([w2, w1], axis=0).T[:64]
    d0 = jnp.where(lower, pltpu.roll(d1, 64, 1), 0.0)
    d3 = jnp.where(lower, 0.0, pltpu.roll(d2, 64, 1))
    return [d.astype(BF16) for d in (d0, d1, d2, d3)]


def put_bands(out_ref, start, blocks, columns):
    for i, block in enumerate(blocks):
        out_ref[start + 64 * i : start + 64 * (i + 1), columns : columns + 128] = block


def prepare_second(first_hbm, second_hbm, coarse_hbm, head_hbm, raw_hbm, *refs):
    (w2_ref, first_ref, coarse_ref, head_ref, raw_ref, rows_ref, second_ref, sems) = refs
    copies = [
        pltpu.make_async_copy(src, dst, sems.at[i])
        for i, (src, dst) in enumerate(
            (
                (second_hbm, second_ref),
                (raw_hbm, raw_ref),
                (first_hbm, first_ref),
                (head_hbm, head_ref),
                (coarse_hbm, coarse_ref),
            )
        )
    ]
    for copy in copies:
        copy.start()

    zeros = jnp.zeros((256, 128), BF16)
    for w in range(4):
        w2_ref[1024 * w : 1024 * w + 256, 128:256] = zeros
        w2_ref[1024 * w + 768 : 1024 * w + 1024, 0:128] = zeros
    copies[0].wait()
    tap_rows(second_ref, rows_ref)
    for w in range(4):
        for dy in range(3):
            taps = []
            for dx in range(3):
                g0, g1, g2 = (
                    rows_ref[64 * t : 64 * (t + 1), :] for t in range(3 * dy + dx, 27, 9)
                )
                taps.append((g0, 0.5 * (g0 + g1 + g2), 0.5 * (g0 - g1 + g2), g2)[w])
            blocks = band(*taps)
            for yy in range(2):
                put_bands(w2_ref, 256 * (4 * w + dy + yy), blocks, 128 * yy)
    for copy in copies[1:]:
        copy.wait()


def prepare_rest(first_ref, coarse_ref, head_ref, w1_ref, wc_ref, wh_ref, rows_ref):
    shape = (256, 27)
    row, lane = iota(shape, 0), iota(shape, 1)
    xo, dz, y = row // 64, (row // 16) % 4, row % 16
    first = jnp.concatenate(
        [first_ref[0, k // 3, k % 3].astype(F32) for k in range(9)], axis=0
    ).astype(BF16)
    parts = []
    for yy in range(2):
        for xx in range(2):
            dy, dx = y - yy, xo - xx
            valid = (dz < 3) & (dy >= 0) & (dy < 3) & (dx >= 0) & (dx < 3)
            pick = jnp.where(valid & (lane == dz * 9 + dy * 3 + dx), 1.0, 0.0).astype(BF16)
            parts.append(dot(pick, first))
    base = jnp.concatenate(parts, axis=1)
    for yp in range(7):
        moved = base if yp == 0 else pltpu.roll(base, 2 * yp, 0)
        w1_ref[:, 256 * yp : 256 * (yp + 1)] = moved.astype(BF16)

    wide = (240, 256)
    row, lane = iota(wide, 0), iota(wide, 1)
    yp, xx, y = row // 48, (row // 24) % 2, row % 8
    o = (row // 8) % 3
    head = head_ref[...].astype(F32)
    tiled = jnp.concatenate([head] * 4, axis=1)
    value = jnp.where(o == 0, tiled[0:1], jnp.where(o == 1, tiled[1:2], tiled[2:3]))
    fine = (y // 2 == yp) & (y % 2 == lane // 128) & (xx == (lane // 64) % 2)
    up = (yp == 4) & (y // 2 == lane // 64)
    wh_ref[...] = jnp.where(fine | up, value, 0.0).astype(BF16)

    tap_rows(coarse_ref, rows_ref)
    zeros = jnp.zeros((128, 128), BF16)
    for dz in range(3):
        for dx in range(3):
            blocks = band(
                *(rows_ref[64 * t : 64 * (t + 1), :] for t in range(9 * dz + dx, 9 * dz + 9, 3))
            )
            start = 384 * (3 * dz + dx)
            for half in range(2):
                put_bands(wc_ref, start + 128 * half, blocks, 128 * half)
            wc_ref[start + 256 : start + 384, 0:128] = zeros
            wc_ref[start : start + 128, 128:256] = zeros


def side_by_side(logits):
    lower = iota((24, 128), 1) < 64
    planes = []
    for half in range(2):
        tile = logits[:, 128 * half : 128 * (half + 1)]
        even, odd = tile[:24], tile[24:]
        planes.append(jnp.where(lower, even, pltpu.roll(odd, 64, 1)))
        planes.append(jnp.where(lower, pltpu.roll(even, 64, 1), odd))
    return planes


def tile_kernel(halo_count, tile_count, counts_hbm, offsets_hbm, raw_ref, *refs):
    ysides = refs[: 1 + (halo_count > 2)]
    refs = refs[len(ysides) :]
    (pair_ref, chain_ref, w1_ref, w2_ref, wc_ref, wh_ref, out_ref) = refs[:7]
    (ext_ref, u_ref, a_ref, s_ref, q_ref, lc_ref, fine_ref, up_ref, pred_ref) = refs[7:16]
    counts_ref, offsets_ref, sems = refs[16:]
    copies = [
        pltpu.make_async_copy(counts_hbm, counts_ref, sems.at[0]),
        pltpu.make_async_copy(offsets_hbm, offsets_ref, sems.at[1]),
    ]
    for copy in copies:
        copy.start()

    halo_index = lax.axis_index("halo")
    gz_index = lax.axis_index("gz")
    tile_index = lax.axis_index("blocks") * 2 + gz_index

    odd_h = halo_index % 2 == 1
    odd_g = gz_index == 1

    def with_rows(own, sides):
        own = own.astype(F32)
        near = sides[0].astype(F32)
        far = sides[1].astype(F32) if len(sides) > 1 else jnp.zeros_like(near)
        below = jnp.where(odd_h, near, far)
        above = jnp.where(odd_h, far, near)
        return jnp.concatenate([below[:, 4:8], own, above[:, 0:4]], axis=1)

    core = with_rows(raw_ref[...], [r[...] for r in ysides])
    pair = with_rows(pair_ref[0], [pair_ref[1 + k] for k in range(len(ysides))])
    chain = with_rows(chain_ref[0], [chain_ref[1 + k] for k in range(len(ysides))])
    edge = jnp.where(odd_g, tile_index == tile_count - 1, tile_index == 0)
    chain = jnp.where(edge, 0.0, chain)
    below = jnp.where(odd_g, pair, chain)
    above = jnp.where(odd_g, chain, pair)
    ext = jnp.concatenate([below, core, above, jnp.zeros((2, 16, 128), F32)], axis=0)
    ext = ext.reshape(26 * 16, 128)
    moved = jnp.where(iota(ext.shape, 1) < 127, pltpu.roll(ext, 127, 1), 0.0)
    ext_ref[0] = ext.astype(BF16).reshape(26, 16, 128)
    ext_ref[1] = moved.astype(BF16).reshape(26, 16, 128)

    row, lane = iota((160, 128), 0), iota((160, 128), 1)
    select = jnp.where(lane == 2 * (row % 80) - 2 + 2 * (row // 80), 1.0, 0.0).astype(BF16)
    for z in range(0, 22, 2):
        around = jnp.concatenate(
            [ext_ref[m, z + d : z + d + 4].reshape(64, 128) for d in range(2) for m in range(2)],
            axis=0,
        )
        u = dot_t(select, around).astype(BF16)
        for d in range(2):
            for m in range(2):
                u_ref[z + d, :, 128 * m : 128 * (m + 1)] = u[
                    80 * m : 80 * (m + 1), 128 * d : 128 * (d + 1)
                ]

    edge_rows, edge_lanes = iota((8, 128), 0), iota((8, 128), 1)
    keep_first = (edge_rows > 0) | (edge_lanes >= 64)
    keep_last = (edge_rows < 1) & (edge_lanes < 64)

    def first_step(k, carry):
        z = 11 * k
        lhs = u_ref[pl.ds(z, 11)].reshape(880, 256)
        for yp in range(7):
            res = jnp.maximum(dot(lhs, w1_ref[:, 256 * yp : 256 * (yp + 1)]), 0.0)
            for d in range(11):
                for yy in range(2):
                    tile = res[80 * d : 80 * d + 72, 128 * yy : 128 * (yy + 1)]
                    head = jnp.where(keep_first, tile[:8], 0.0)
                    tail = jnp.where(keep_last, tile[64:], 0.0)
                    tile = jnp.concatenate([head, tile[8:64], tail], axis=0)
                    a_ref[z + d, yy, yp, :, 0:128] = tile[:64].astype(BF16)
                    after = pltpu.roll(tile, 71, 0)[:64]
                    a_ref[z + d, yy, yp, :, 128:256] = after.astype(BF16)
        return carry

    lax.fori_loop(0, 2, first_step, 0)

    lower_half = iota((64, 128), 1) < 64

    def second_step(k, carry):
        z = 4 * k
        products = []
        for w, (i, j) in enumerate(((0, 2), (1, 2), (2, 1), (1, 3))):
            mixed = []
            for p in range(2):
                first, second = a_ref[z + 2 * p + i], a_ref[z + 2 * p + j]
                mixed.append(first + second if w == 1 else first - second)
            product = None
            for y in range(4):
                lhs = jnp.concatenate(
                    [m[y % 2, y // 2 : y // 2 + 6].reshape(384, 256) for m in mixed], axis=0
                )
                at = 256 * (4 * w + y)
                term = dot(lhs, w2_ref[at : at + 256, :])
                product = term if product is None else product + term
            products.append(product)
        m0, m1, m2, m3 = products
        acts = [m0 + m1 + m2, m1 - m2 - m3]
        acts = [jnp.maximum(act, 0.0).astype(BF16).reshape(2, 6, 64, 256) for act in acts]
        planes = [acts[d % 2][d // 2] for d in range(4)]
        for d, plane in enumerate(planes):
            s_ref[z + d] = plane[1:5]
        for d, plane in enumerate(planes):
            full = plane.astype(F32)
            both = full[:, :, :128] + full[:, :, 128:]
            for j in range(3):
                even, odd = both[2 * j], both[2 * j + 1]
                even = even + pltpu.roll(even, 64, 1)
                odd = odd + pltpu.roll(odd, 64, 1)
                q_ref[z + d, j] = jnp.where(lower_half, even, odd)
        return carry

    lax.fori_loop(0, 5, second_step, 0)

    for z in range(2, 18, 4):
        logits = None
        for yp in range(4):
            term = dot_t(wh_ref[48 * yp : 48 * (yp + 1), :], s_ref[z : z + 4, yp].reshape(256, 256))
            logits = term if logits is None else logits + term
        for d, plane in enumerate(side_by_side(logits)):
            fine_ref[z - 2 + d] = plane

    for copy in copies:
        copy.wait()
    slots = counts_ref.shape[2]
    total = jnp.int32(0)
    anchors = [jnp.int32(0)] * MOST
    for s in range(slots):
        dense = counts_ref[0, 0, s] >= MINC
        for j in range(MOST):
            anchors[j] = jnp.where(dense & (total == j), offsets_ref[0, 0, s], anchors[j])
        total = total + dense.astype(jnp.int32)

    rows64 = iota((64, 128), 0)
    for j in range(MOST):
        for k in range(6):
            for m in range(3):
                z = anchors[j] + 2 * k
                mean = (q_ref[z, m] + q_ref[z + 1, m]) * 0.125
                before = jnp.where(rows64 == 0, 0.0, pltpu.roll(mean, 1, 0))
                after = jnp.where(rows64 == 63, 0.0, pltpu.roll(mean, 63, 0))
                for dx, value in enumerate((before, mean, after)):
                    at = 384 * dx + 128 * m
                    lc_ref[j, k, :, at : at + 128] = value.astype(BF16)

    coarse = None
    for dz in range(3):
        lhs = lc_ref[:, dz : dz + 4].reshape(MOST * 256, 1152)
        term = dot(lhs, wc_ref[1152 * dz : 1152 * (dz + 1), :])
        coarse = term if coarse is None else coarse + term
    coarse = jnp.maximum(coarse, 0.0).astype(BF16)
    for j in range(MOST):
        logits = dot_t(wh_ref[192:240, :], coarse[256 * j : 256 * (j + 1)])
        for k, plane in enumerate(side_by_side(logits)):
            up_ref[j, k] = plane

    row, lane = iota((128, 128), 0), iota((128, 128), 1)
    order = jnp.where(lane == 2 * (row % 64) + row // 64, 1.0, 0.0).astype(BF16)
    preds = []
    for j in range(MOST):
        for u in range(CORE):
            logits = fine_ref[anchors[j] + u] + up_ref[j, u // 2]
            preds.append(jax.nn.sigmoid(logits))
    ordered = dot(jnp.concatenate(preds, axis=0).astype(BF16), order)
    pred_ref[...] = ordered.reshape(MOST, CORE, 3, 8, 128)

    for z in range(16):
        cover = jnp.float32(0.0)
        value = jnp.zeros((3, 8, 128), F32)
        for j in range(MOST):
            u = z - anchors[j]
            uf = u.astype(F32)
            tent = (uf + 1.0) * (CORE - uf) / 20.0
            inside = (j < total) & (u >= 0) & (u < CORE)
            tent = jnp.where(inside, tent, 0.0)
            cover = cover + tent
            value = value + pred_ref[j, jnp.clip(u, 0, CORE - 1)] * tent
        value = value / jnp.maximum(jnp.full((8, 128), cover, F32), 1.0)
        for c in range(3):
            out_ref[c, z] = value[c]


def neighbour_pairs(count, first):
    pairs = []
    for i in range(first, count - 1, 2):
        pairs += [(i, i + 1), (i + 1, i)]
    return pairs


def chain_pairs(tile_count, halo_count):
    def device(tile, h):
        return (tile // 2 * halo_count + h) * 2 + tile % 2

    pairs = []
    for h in range(halo_count):
        pairs += [(device(a, h), device(b, h)) for a, b in neighbour_pairs(tile_count, 1)]
        pairs += [(device(end, h), device(end, h ^ 1)) for end in (0, tile_count - 1)]
    return pairs


def local(raw_volume, tissue_counts, patch_core_offsets, w_first, w_second, w_coarse, w_head):
    halo_count = lax.axis_size("halo")
    tile_count = lax.axis_size("blocks") * lax.axis_size("gz")
    vmem = pl.BlockSpec(memory_space=pltpu.VMEM)
    hbm = pl.BlockSpec(memory_space=HBM)

    ysides = [lax.ppermute(raw_volume, "halo", neighbour_pairs(halo_count, 0))]
    if halo_count > 2:
        ysides.append(lax.ppermute(raw_volume, "halo", neighbour_pairs(halo_count, 1)))

    first_taps = jnp.transpose(w_first, (1, 2, 3, 4, 0))
    held = [first_taps, w_coarse, w_head, raw_volume]
    sources = [first_taps, w_second, w_coarse, w_head, raw_volume]
    w2, first, coarse, head, raw = pl.pallas_call(
        prepare_second,
        out_shape=[jax.ShapeDtypeStruct((4096, 256), BF16)]
        + [jax.ShapeDtypeStruct(x.shape, BF16) for x in held],
        in_specs=[hbm] * 5,
        out_specs=[vmem] * 5,
        scratch_shapes=[
            pltpu.VMEM((27 * 64, 128), F32),
            pltpu.VMEM(w_second.shape, BF16),
            pltpu.SemaphoreType.DMA((5,)),
        ],
        compiler_params=pltpu.CompilerParams(vmem_limit_bytes=24 << 20),
        cost_estimate=pl.CostEstimate(flops=1 << 20, bytes_accessed=8 << 20, transcendentals=0),
    )(*(pltpu.with_memory_space_constraint(x, HBM) for x in sources))

    stack = jnp.stack([raw] + ysides)
    odd = lax.axis_index("gz") == 1
    first_layers, last_layers = stack[:, :MARGIN], stack[:, -MARGIN:]
    pair = lax.ppermute(jnp.where(odd, first_layers, last_layers), "gz", [(0, 1), (1, 0)])
    chain = lax.ppermute(
        jnp.where(odd, last_layers, first_layers),
        ("blocks", "halo", "gz"),
        chain_pairs(tile_count, halo_count),
    )

    w1, wc, wh = pl.pallas_call(
        prepare_rest,
        out_shape=[
            jax.ShapeDtypeStruct((256, 1792), BF16),
            jax.ShapeDtypeStruct((3456, 256), BF16),
            jax.ShapeDtypeStruct((240, 256), BF16),
        ],
        in_specs=[vmem] * 3,
        out_specs=[vmem] * 3,
        scratch_shapes=[pltpu.VMEM((27 * 64, 128), F32)],
        compiler_params=pltpu.CompilerParams(vmem_limit_bytes=16 << 20),
        cost_estimate=pl.CostEstimate(flops=1 << 20, bytes_accessed=6 << 20, transcendentals=0),
    )(first, coarse, head)

    def body(*refs):
        tile_kernel(halo_count, tile_count, *refs)

    return pl.pallas_call(
        body,
        out_shape=jax.ShapeDtypeStruct((3, 16, 8, 128), F32),
        in_specs=[hbm, hbm] + [vmem] * (7 + len(ysides)),
        out_specs=vmem,
        scratch_shapes=[
            pltpu.VMEM((2, 26, 16, 128), BF16),
            pltpu.VMEM((22, 80, 256), BF16),
            pltpu.VMEM((22, 2, 7, 64, 256), BF16),
            pltpu.VMEM((20, 4, 64, 256), BF16),
            pltpu.VMEM((20, 3, 64, 128), F32),
            pltpu.VMEM((MOST, 6, 64, 1152), BF16),
            pltpu.VMEM((16, 24, 128), F32),
            pltpu.VMEM((MOST, 4, 24, 128), F32),
            pltpu.VMEM((MOST, CORE, 3, 8, 128), F32),
            pltpu.SMEM(tissue_counts.shape, jnp.int32),
            pltpu.SMEM(patch_core_offsets.shape, jnp.int32),
            pltpu.SemaphoreType.DMA((2,)),
        ],
        compiler_params=pltpu.CompilerParams(vmem_limit_bytes=40 << 20),
        cost_estimate=pl.CostEstimate(flops=16 << 30, bytes_accessed=5 << 20, transcendentals=0),
    )(
        pltpu.with_memory_space_constraint(tissue_counts, HBM),
        pltpu.with_memory_space_constraint(patch_core_offsets, HBM),
        raw,
        *ysides,
        pair,
        chain,
        w1,
        w2,
        wc,
        wh,
    )


def solution(mesh):
    in_specs = (
        P(("groups", "blocks", "gz"), "halo", None),
        P(("groups", "blocks", "gz"), "halo", None),
        P(("groups", "blocks", "gz"), "halo", None),
        P(),
        P(),
        P(),
        P(),
    )
    out_specs = P(None, ("groups", "blocks", "gz"), "halo", None)
    return jax.shard_map(local, mesh=mesh, in_specs=in_specs, out_specs=out_specs, check_vma=False)
```

```python
import jax
import jax.numpy as jnp
from jax import lax
from jax.experimental import pallas as pl
from jax.experimental.pallas import tpu as pltpu
from jax.sharding import PartitionSpec as P

CORE = 8
MARGIN = 4
MOST = 3
MINC = 4096
F32 = jnp.float32
BF16 = jnp.bfloat16
HBM = pltpu.HBM


def dot(a, b):
    return lax.dot_general(a, b, (((1,), (0,)), ((), ())), preferred_element_type=F32)


def dot_t(a, b):
    return lax.dot_general(a, b, (((1,), (1,)), ((), ())), preferred_element_type=F32)


def iota(shape, dim):
    return lax.broadcasted_iota(jnp.int32, shape, dim)


def tap_rows(flat_ref, rows_ref):
    taps = flat_ref.shape[0]
    for j in range(32):
        block = flat_ref[:, 128 * j : 128 * (j + 1)].astype(F32)
        rows_ref[pl.ds(2 * j, taps, stride=64), :] = block
        rows_ref[pl.ds(2 * j + 1, taps, stride=64), :] = pltpu.roll(block, 64, 1)


def band(w0, w1, w2):
    lower = iota((64, 128), 1) < 64
    d1 = jnp.concatenate([w1, w0], axis=0).T[:64]
    d2 = jnp.concatenate([w2, w1], axis=0).T[:64]
    d0 = jnp.where(lower, pltpu.roll(d1, 64, 1), 0.0)
    d3 = jnp.where(lower, 0.0, pltpu.roll(d2, 64, 1))
    return [d.astype(BF16) for d in (d0, d1, d2, d3)]


def put_bands(out_ref, start, blocks, columns):
    for i, block in enumerate(blocks):
        out_ref[start + 64 * i : start + 64 * (i + 1), columns : columns + 128] = block


def prepare_second(first_hbm, second_hbm, coarse_hbm, head_hbm, raw_hbm, *refs):
    (w2_ref, first_ref, coarse_ref, head_ref, raw_ref, rows_ref, second_ref, sems) = refs
    copies = [
        pltpu.make_async_copy(src, dst, sems.at[i])
        for i, (src, dst) in enumerate(
            (
                (second_hbm, second_ref),
                (raw_hbm, raw_ref),
                (first_hbm, first_ref),
                (head_hbm, head_ref),
                (coarse_hbm, coarse_ref),
            )
        )
    ]
    for copy in copies:
        copy.start()

    zeros = jnp.zeros((256, 128), BF16)
    for w in range(4):
        w2_ref[1024 * w : 1024 * w + 256, 128:256] = zeros
        w2_ref[1024 * w + 768 : 1024 * w + 1024, 0:128] = zeros
    copies[0].wait()
    tap_rows(second_ref, rows_ref)
    for w in range(4):
        for dy in range(3):
            taps = []
            for dx in range(3):
                g0, g1, g2 = (
                    rows_ref[64 * t : 64 * (t + 1), :] for t in range(3 * dy + dx, 27, 9)
                )
                taps.append((g0, 0.5 * (g0 + g1 + g2), 0.5 * (g0 - g1 + g2), g2)[w])
            blocks = band(*taps)
            for yy in range(2):
                put_bands(w2_ref, 256 * (4 * w + dy + yy), blocks, 128 * yy)
    for copy in copies[1:]:
        copy.wait()


def prepare_rest(first_ref, coarse_ref, head_ref, w1_ref, wc_ref, wh_ref, rows_ref):
    shape = (256, 27)
    row, lane = iota(shape, 0), iota(shape, 1)
    xo, dz, y = row // 64, (row // 16) % 4, row % 16
    first = jnp.concatenate(
        [first_ref[0, k // 3, k % 3].astype(F32) for k in range(9)], axis=0
    ).astype(BF16)
    parts = []
    for yy in range(2):
        for xx in range(2):
            dy, dx = y - yy, xo - xx
            valid = (dz < 3) & (dy >= 0) & (dy < 3) & (dx >= 0) & (dx < 3)
            pick = jnp.where(valid & (lane == dz * 9 + dy * 3 + dx), 1.0, 0.0).astype(BF16)
            parts.append(dot(pick, first))
    base = jnp.concatenate(parts, axis=1)
    for yp in range(7):
        moved = base if yp == 0 else pltpu.roll(base, 2 * yp, 0)
        w1_ref[:, 256 * yp : 256 * (yp + 1)] = moved.astype(BF16)

    wide = (240, 256)
    row, lane = iota(wide, 0), iota(wide, 1)
    yp, xx, y = row // 48, (row // 24) % 2, row % 8
    o = (row // 8) % 3
    head = head_ref[...].astype(F32)
    tiled = jnp.concatenate([head] * 4, axis=1)
    value = jnp.where(o == 0, tiled[0:1], jnp.where(o == 1, tiled[1:2], tiled[2:3]))
    fine = (y // 2 == yp) & (y % 2 == lane // 128) & (xx == (lane // 64) % 2)
    up = (yp == 4) & (y // 2 == lane // 64)
    wh_ref[...] = jnp.where(fine | up, value, 0.0).astype(BF16)

    tap_rows(coarse_ref, rows_ref)
    zeros = jnp.zeros((128, 128), BF16)
    for dz in range(3):
        for dx in range(3):
            blocks = band(
                *(rows_ref[64 * t : 64 * (t + 1), :] for t in range(9 * dz + dx, 9 * dz + 9, 3))
            )
            start = 384 * (3 * dz + dx)
            for half in range(2):
                put_bands(wc_ref, start + 128 * half, blocks, 128 * half)
            wc_ref[start + 256 : start + 384, 0:128] = zeros
            wc_ref[start : start + 128, 128:256] = zeros


def side_by_side(logits):
    lower = iota((24, 128), 1) < 64
    planes = []
    for half in range(2):
        tile = logits[:, 128 * half : 128 * (half + 1)]
        even, odd = tile[:24], tile[24:]
        planes.append(jnp.where(lower, even, pltpu.roll(odd, 64, 1)))
        planes.append(jnp.where(lower, pltpu.roll(even, 64, 1), odd))
    return planes


def tile_kernel(halo_count, tile_count, counts_hbm, offsets_hbm, raw_ref, *refs):
    ysides = refs[: 1 + (halo_count > 2)]
    refs = refs[len(ysides) :]
    (pair_ref, chain_ref, w1_ref, w2_ref, wc_ref, wh_ref, out_ref) = refs[:7]
    (ext_ref, u_ref, a_ref, s_ref, q_ref, lc_ref, fine_ref, up_ref, pred_ref) = refs[7:16]
    counts_ref, offsets_ref, sems = refs[16:]
    copies = [
        pltpu.make_async_copy(counts_hbm, counts_ref, sems.at[0]),
        pltpu.make_async_copy(offsets_hbm, offsets_ref, sems.at[1]),
    ]
    for copy in copies:
        copy.start()

    halo_index = lax.axis_index("halo")
    gz_index = lax.axis_index("gz")
    tile_index = lax.axis_index("blocks") * 2 + gz_index

    odd_h = halo_index % 2 == 1
    odd_g = gz_index == 1

    def with_rows(own, sides):
        own = own.astype(F32)
        near = sides[0].astype(F32)
        far = sides[1].astype(F32) if len(sides) > 1 else jnp.zeros_like(near)
        below = jnp.where(odd_h, near, far)
        above = jnp.where(odd_h, far, near)
        return jnp.concatenate([below[:, 4:8], own, above[:, 0:4]], axis=1)

    core = with_rows(raw_ref[...], [r[...] for r in ysides])
    pair = with_rows(pair_ref[0], [pair_ref[1 + k] for k in range(len(ysides))])
    chain = with_rows(chain_ref[0], [chain_ref[1 + k] for k in range(len(ysides))])
    edge = jnp.where(odd_g, tile_index == tile_count - 1, tile_index == 0)
    chain = jnp.where(edge, 0.0, chain)
    below = jnp.where(odd_g, pair, chain)
    above = jnp.where(odd_g, chain, pair)
    ext = jnp.concatenate([below, core, above, jnp.zeros((2, 16, 128), F32)], axis=0)
    ext = ext.reshape(26 * 16, 128)
    moved = jnp.where(iota(ext.shape, 1) < 127, pltpu.roll(ext, 127, 1), 0.0)
    ext_ref[0] = ext.astype(BF16).reshape(26, 16, 128)
    ext_ref[1] = moved.astype(BF16).reshape(26, 16, 128)

    row, lane = iota((160, 128), 0), iota((160, 128), 1)
    select = jnp.where(lane == 2 * (row % 80) - 2 + 2 * (row // 80), 1.0, 0.0).astype(BF16)
    for z in range(0, 22, 2):
        around = jnp.concatenate(
            [ext_ref[m, z + d : z + d + 4].reshape(64, 128) for d in range(2) for m in range(2)],
            axis=0,
        )
        u = dot_t(select, around).astype(BF16)
        for d in range(2):
            for m in range(2):
                u_ref[z + d, :, 128 * m : 128 * (m + 1)] = u[
                    80 * m : 80 * (m + 1), 128 * d : 128 * (d + 1)
                ]

    edge_rows, edge_lanes = iota((8, 128), 0), iota((8, 128), 1)
    keep_first = (edge_rows > 0) | (edge_lanes >= 64)
    keep_last = (edge_rows < 1) & (edge_lanes < 64)

    def first_step(k, carry):
        z = 11 * k
        lhs = u_ref[pl.ds(z, 11)].reshape(880, 256)
        for yp in range(7):
            res = jnp.maximum(dot(lhs, w1_ref[:, 256 * yp : 256 * (yp + 1)]), 0.0)
            for d in range(11):
                for yy in range(2):
                    tile = res[80 * d : 80 * d + 72, 128 * yy : 128 * (yy + 1)]
                    head = jnp.where(keep_first, tile[:8], 0.0)
                    tail = jnp.where(keep_last, tile[64:], 0.0)
                    tile = jnp.concatenate([head, tile[8:64], tail], axis=0)
                    a_ref[z + d, yy, yp, :, 0:128] = tile[:64].astype(BF16)
                    after = pltpu.roll(tile, 71, 0)[:64]
                    a_ref[z + d, yy, yp, :, 128:256] = after.astype(BF16)
        return carry

    lax.fori_loop(0, 2, first_step, 0)

    lower_half = iota((64, 128), 1) < 64

    def finish(z, act):
        act = jnp.maximum(act, 0.0).astype(BF16).reshape(6, 64, 256)
        s_ref[z] = act[1:5]
        full = act.astype(F32)
        both = full[:, :, :128] + full[:, :, 128:]
        for j in range(3):
            even, odd = both[2 * j], both[2 * j + 1]
            even = even + pltpu.roll(even, 64, 1)
            odd = odd + pltpu.roll(odd, 64, 1)
            q_ref[z, j] = jnp.where(lower_half, even, odd)

    def second_step(k, carry):
        for p in range(5):
            z = 10 * k + 2 * p
            products = []
            for w, (i, j) in enumerate(((0, 2), (1, 2), (2, 1), (1, 3))):
                first, second = a_ref[z + i], a_ref[z + j]
                mixed = first + second if w == 1 else first - second
                product = None
                for y in range(4):
                    lhs = mixed[y % 2, y // 2 : y // 2 + 6].reshape(384, 256)
                    at = 256 * (4 * w + y)
                    term = dot(lhs, w2_ref[at : at + 256, :])
                    product = term if product is None else product + term
                products.append(product)
            m0, m1, m2, m3 = products
            finish(z, m0 + m1 + m2)
            finish(z + 1, m1 - m2 - m3)
        return carry

    lax.fori_loop(0, 2, second_step, 0)

    for z in range(2, 18, 4):
        logits = None
        for yp in range(4):
            term = dot_t(wh_ref[48 * yp : 48 * (yp + 1), :], s_ref[z : z + 4, yp].reshape(256, 256))
            logits = term if logits is None else logits + term
        for d, plane in enumerate(side_by_side(logits)):
            fine_ref[z - 2 + d] = plane

    for copy in copies:
        copy.wait()
    slots = counts_ref.shape[2]
    total = jnp.int32(0)
    anchors = [jnp.int32(0)] * MOST
    for s in range(slots):
        dense = counts_ref[0, 0, s] >= MINC
        for j in range(MOST):
            anchors[j] = jnp.where(dense & (total == j), offsets_ref[0, 0, s], anchors[j])
        total = total + dense.astype(jnp.int32)

    rows64 = iota((64, 128), 0)
    for j in range(MOST):
        for k in range(6):
            for m in range(3):
                z = anchors[j] + 2 * k
                mean = (q_ref[z, m] + q_ref[z + 1, m]) * 0.125
                before = jnp.where(rows64 == 0, 0.0, pltpu.roll(mean, 1, 0))
                after = jnp.where(rows64 == 63, 0.0, pltpu.roll(mean, 63, 0))
                for dx, value in enumerate((before, mean, after)):
                    at = 384 * dx + 128 * m
                    lc_ref[j, k, :, at : at + 128] = value.astype(BF16)

    coarse = None
    for dz in range(3):
        lhs = lc_ref[:, dz : dz + 4].reshape(MOST * 256, 1152)
        term = dot(lhs, wc_ref[1152 * dz : 1152 * (dz + 1), :])
        coarse = term if coarse is None else coarse + term
    coarse = jnp.maximum(coarse, 0.0).astype(BF16)
    for j in range(MOST):
        logits = dot_t(wh_ref[192:240, :], coarse[256 * j : 256 * (j + 1)])
        for k, plane in enumerate(side_by_side(logits)):
            up_ref[j, k] = plane

    row, lane = iota((128, 128), 0), iota((128, 128), 1)
    order = jnp.where(lane == 2 * (row % 64) + row // 64, 1.0, 0.0).astype(BF16)
    preds = []
    for j in range(MOST):
        for u in range(CORE):
            logits = fine_ref[anchors[j] + u] + up_ref[j, u // 2]
            preds.append(jax.nn.sigmoid(logits))
    ordered = dot(jnp.concatenate(preds, axis=0).astype(BF16), order)
    pred_ref[...] = ordered.reshape(MOST, CORE, 3, 8, 128)

    for z in range(16):
        cover = jnp.float32(0.0)
        value = jnp.zeros((3, 8, 128), F32)
        for j in range(MOST):
            u = z - anchors[j]
            uf = u.astype(F32)
            tent = (uf + 1.0) * (CORE - uf) / 20.0
            inside = (j < total) & (u >= 0) & (u < CORE)
            tent = jnp.where(inside, tent, 0.0)
            cover = cover + tent
            value = value + pred_ref[j, jnp.clip(u, 0, CORE - 1)] * tent
        value = value / jnp.maximum(jnp.full((8, 128), cover, F32), 1.0)
        for c in range(3):
            out_ref[c, z] = value[c]


def neighbour_pairs(count, first):
    pairs = []
    for i in range(first, count - 1, 2):
        pairs += [(i, i + 1), (i + 1, i)]
    return pairs


def chain_pairs(tile_count, halo_count):
    def device(tile, h):
        return (tile // 2 * halo_count + h) * 2 + tile % 2

    pairs = []
    for h in range(halo_count):
        pairs += [(device(a, h), device(b, h)) for a, b in neighbour_pairs(tile_count, 1)]
        pairs += [(device(end, h), device(end, h ^ 1)) for end in (0, tile_count - 1)]
    return pairs


def local(raw_volume, tissue_counts, patch_core_offsets, w_first, w_second, w_coarse, w_head):
    halo_count = lax.axis_size("halo")
    tile_count = lax.axis_size("blocks") * lax.axis_size("gz")
    vmem = pl.BlockSpec(memory_space=pltpu.VMEM)
    hbm = pl.BlockSpec(memory_space=HBM)

    ysides = [lax.ppermute(raw_volume, "halo", neighbour_pairs(halo_count, 0))]
    if halo_count > 2:
        ysides.append(lax.ppermute(raw_volume, "halo", neighbour_pairs(halo_count, 1)))

    first_taps = jnp.transpose(w_first, (1, 2, 3, 4, 0))
    held = [first_taps, w_coarse, w_head, raw_volume]
    sources = [first_taps, w_second, w_coarse, w_head, raw_volume]
    w2, first, coarse, head, raw = pl.pallas_call(
        prepare_second,
        out_shape=[jax.ShapeDtypeStruct((4096, 256), BF16)]
        + [jax.ShapeDtypeStruct(x.shape, BF16) for x in held],
        in_specs=[hbm] * 5,
        out_specs=[vmem] * 5,
        scratch_shapes=[
            pltpu.VMEM((27 * 64, 128), F32),
            pltpu.VMEM(w_second.shape, BF16),
            pltpu.SemaphoreType.DMA((5,)),
        ],
        compiler_params=pltpu.CompilerParams(vmem_limit_bytes=24 << 20),
        cost_estimate=pl.CostEstimate(flops=1 << 20, bytes_accessed=8 << 20, transcendentals=0),
    )(*(pltpu.with_memory_space_constraint(x, HBM) for x in sources))

    stack = jnp.stack([raw] + ysides)
    odd = lax.axis_index("gz") == 1
    first_layers, last_layers = stack[:, :MARGIN], stack[:, -MARGIN:]
    pair = lax.ppermute(jnp.where(odd, first_layers, last_layers), "gz", [(0, 1), (1, 0)])
    chain = lax.ppermute(
        jnp.where(odd, last_layers, first_layers),
        ("blocks", "halo", "gz"),
        chain_pairs(tile_count, halo_count),
    )

    w1, wc, wh = pl.pallas_call(
        prepare_rest,
        out_shape=[
            jax.ShapeDtypeStruct((256, 1792), BF16),
            jax.ShapeDtypeStruct((3456, 256), BF16),
            jax.ShapeDtypeStruct((240, 256), BF16),
        ],
        in_specs=[vmem] * 3,
        out_specs=[vmem] * 3,
        scratch_shapes=[pltpu.VMEM((27 * 64, 128), F32)],
        compiler_params=pltpu.CompilerParams(vmem_limit_bytes=16 << 20),
        cost_estimate=pl.CostEstimate(flops=1 << 20, bytes_accessed=6 << 20, transcendentals=0),
    )(first, coarse, head)

    def body(*refs):
        tile_kernel(halo_count, tile_count, *refs)

    return pl.pallas_call(
        body,
        out_shape=jax.ShapeDtypeStruct((3, 16, 8, 128), F32),
        in_specs=[hbm, hbm] + [vmem] * (7 + len(ysides)),
        out_specs=vmem,
        scratch_shapes=[
            pltpu.VMEM((2, 26, 16, 128), BF16),
            pltpu.VMEM((22, 80, 256), BF16),
            pltpu.VMEM((22, 2, 7, 64, 256), BF16),
            pltpu.VMEM((20, 4, 64, 256), BF16),
            pltpu.VMEM((20, 3, 64, 128), F32),
            pltpu.VMEM((MOST, 6, 64, 1152), BF16),
            pltpu.VMEM((16, 24, 128), F32),
            pltpu.VMEM((MOST, 4, 24, 128), F32),
            pltpu.VMEM((MOST, CORE, 3, 8, 128), F32),
            pltpu.SMEM(tissue_counts.shape, jnp.int32),
            pltpu.SMEM(patch_core_offsets.shape, jnp.int32),
            pltpu.SemaphoreType.DMA((2,)),
        ],
        compiler_params=pltpu.CompilerParams(vmem_limit_bytes=40 << 20),
        cost_estimate=pl.CostEstimate(flops=16 << 30, bytes_accessed=5 << 20, transcendentals=0),
    )(
        pltpu.with_memory_space_constraint(tissue_counts, HBM),
        pltpu.with_memory_space_constraint(patch_core_offsets, HBM),
        raw,
        *ysides,
        pair,
        chain,
        w1,
        w2,
        wc,
        wh,
    )


def solution(mesh):
    in_specs = (
        P(("groups", "blocks", "gz"), "halo", None),
        P(("groups", "blocks", "gz"), "halo", None),
        P(("groups", "blocks", "gz"), "halo", None),
        P(),
        P(),
        P(),
        P(),
    )
    out_specs = P(None, ("groups", "blocks", "gz"), "halo", None)
    return jax.shard_map(local, mesh=mesh, in_specs=in_specs, out_specs=out_specs, check_vma=False)
```

```python
import jax
import jax.numpy as jnp
from jax import lax
from jax.experimental import pallas as pl
from jax.experimental.pallas import tpu as pltpu
from jax.sharding import PartitionSpec as P

CORE = 8
MARGIN = 4
MOST = 3
MINC = 4096
F32 = jnp.float32
BF16 = jnp.bfloat16
HBM = pltpu.HBM


def dot(a, b):
    return lax.dot_general(a, b, (((1,), (0,)), ((), ())), preferred_element_type=F32)


def dot_t(a, b):
    return lax.dot_general(a, b, (((1,), (1,)), ((), ())), preferred_element_type=F32)


def iota(shape, dim):
    return lax.broadcasted_iota(jnp.int32, shape, dim)


def tap_rows(flat_ref, rows_ref):
    taps = flat_ref.shape[0]
    for j in range(32):
        block = flat_ref[:, 128 * j : 128 * (j + 1)].astype(F32)
        rows_ref[pl.ds(2 * j, taps, stride=64), :] = block
        rows_ref[pl.ds(2 * j + 1, taps, stride=64), :] = pltpu.roll(block, 64, 1)


def band(w0, w1, w2):
    lower = iota((64, 128), 1) < 64
    d1 = jnp.concatenate([w1, w0], axis=0).T[:64]
    d2 = jnp.concatenate([w2, w1], axis=0).T[:64]
    d0 = jnp.where(lower, pltpu.roll(d1, 64, 1), 0.0)
    d3 = jnp.where(lower, 0.0, pltpu.roll(d2, 64, 1))
    return [d.astype(BF16) for d in (d0, d1, d2, d3)]


def put_bands(out_ref, start, blocks, columns):
    for i, block in enumerate(blocks):
        out_ref[start + 64 * i : start + 64 * (i + 1), columns : columns + 128] = block


def prepare_second(first_hbm, second_hbm, coarse_hbm, head_hbm, raw_hbm, *refs):
    (w2_ref, first_ref, coarse_ref, head_ref, raw_ref, rows_ref, second_ref, sems) = refs
    copies = [
        pltpu.make_async_copy(src, dst, sems.at[i])
        for i, (src, dst) in enumerate(
            (
                (second_hbm, second_ref),
                (raw_hbm, raw_ref),
                (first_hbm, first_ref),
                (head_hbm, head_ref),
                (coarse_hbm, coarse_ref),
            )
        )
    ]
    for copy in copies:
        copy.start()

    zeros = jnp.zeros((256, 128), BF16)
    for w in range(4):
        w2_ref[1024 * w : 1024 * w + 256, 128:256] = zeros
        w2_ref[1024 * w + 768 : 1024 * w + 1024, 0:128] = zeros
    copies[0].wait()
    tap_rows(second_ref, rows_ref)
    for w in range(4):
        for dy in range(3):
            taps = []
            for dx in range(3):
                g0, g1, g2 = (
                    rows_ref[64 * t : 64 * (t + 1), :] for t in range(3 * dy + dx, 27, 9)
                )
                taps.append((g0, 0.5 * (g0 + g1 + g2), 0.5 * (g0 - g1 + g2), g2)[w])
            blocks = band(*taps)
            for yy in range(2):
                put_bands(w2_ref, 256 * (4 * w + dy + yy), blocks, 128 * yy)
    for copy in copies[1:]:
        copy.wait()


def prepare_rest(first_ref, coarse_ref, head_ref, w1_ref, wc_ref, wh_ref, rows_ref):
    shape = (256, 27)
    row, lane = iota(shape, 0), iota(shape, 1)
    xo, dz, y = row // 64, (row // 16) % 4, row % 16
    first = jnp.concatenate(
        [first_ref[0, k // 3, k % 3].astype(F32) for k in range(9)], axis=0
    ).astype(BF16)
    parts = []
    for yy in range(2):
        for xx in range(2):
            dy, dx = y - yy, xo - xx
            valid = (dz < 3) & (dy >= 0) & (dy < 3) & (dx >= 0) & (dx < 3)
            pick = jnp.where(valid & (lane == dz * 9 + dy * 3 + dx), 1.0, 0.0).astype(BF16)
            parts.append(dot(pick, first))
    base = jnp.concatenate(parts, axis=1)
    for yp in range(7):
        moved = base if yp == 0 else pltpu.roll(base, 2 * yp, 0)
        w1_ref[:, 256 * yp : 256 * (yp + 1)] = moved.astype(BF16)

    wide = (240, 256)
    row, lane = iota(wide, 0), iota(wide, 1)
    yp, xx, y = row // 48, (row // 24) % 2, row % 8
    o = (row // 8) % 3
    head = head_ref[...].astype(F32)
    tiled = jnp.concatenate([head] * 4, axis=1)
    value = jnp.where(o == 0, tiled[0:1], jnp.where(o == 1, tiled[1:2], tiled[2:3]))
    fine = (y // 2 == yp) & (y % 2 == lane // 128) & (xx == (lane // 64) % 2)
    up = (yp == 4) & (y // 2 == lane // 64)
    wh_ref[...] = jnp.where(fine | up, value, 0.0).astype(BF16)

    tap_rows(coarse_ref, rows_ref)
    zeros = jnp.zeros((128, 128), BF16)
    for dz in range(3):
        for dx in range(3):
            blocks = band(
                *(rows_ref[64 * t : 64 * (t + 1), :] for t in range(9 * dz + dx, 9 * dz + 9, 3))
            )
            start = 384 * (3 * dz + dx)
            for half in range(2):
                put_bands(wc_ref, start + 128 * half, blocks, 128 * half)
            wc_ref[start + 256 : start + 384, 0:128] = zeros
            wc_ref[start : start + 128, 128:256] = zeros


def side_by_side(logits):
    lower = iota((24, 128), 1) < 64
    planes = []
    for half in range(2):
        tile = logits[:, 128 * half : 128 * (half + 1)]
        even, odd = tile[:24], tile[24:]
        planes.append(jnp.where(lower, even, pltpu.roll(odd, 64, 1)))
        planes.append(jnp.where(lower, pltpu.roll(even, 64, 1), odd))
    return planes


def tile_kernel(halo_count, tile_count, counts_hbm, offsets_hbm, raw_ref, *refs):
    ysides = refs[: 1 + (halo_count > 2)]
    refs = refs[len(ysides) :]
    (pair_ref, chain_ref, w1_ref, w2_ref, wc_ref, wh_ref, out_ref) = refs[:7]
    (ext_ref, u_ref, a_ref, s_ref, q_ref, lc_ref, fine_ref, up_ref, pred_ref) = refs[7:16]
    counts_ref, offsets_ref, sems = refs[16:]
    copies = [
        pltpu.make_async_copy(counts_hbm, counts_ref, sems.at[0]),
        pltpu.make_async_copy(offsets_hbm, offsets_ref, sems.at[1]),
    ]
    for copy in copies:
        copy.start()

    halo_index = lax.axis_index("halo")
    gz_index = lax.axis_index("gz")
    tile_index = lax.axis_index("blocks") * 2 + gz_index

    odd_h = halo_index % 2 == 1
    odd_g = gz_index == 1
    once = jnp.minimum(tile_index + 1, 1)

    def with_rows(own, sides):
        own = own.astype(F32)
        near = sides[0].astype(F32)
        far = sides[1].astype(F32) if len(sides) > 1 else jnp.zeros_like(near)
        below = jnp.where(odd_h, near, far)
        above = jnp.where(odd_h, far, near)
        return jnp.concatenate([below[:, 4:8], own, above[:, 0:4]], axis=1)

    core = with_rows(raw_ref[...], [r[...] for r in ysides])
    pair = with_rows(pair_ref[0], [pair_ref[1 + k] for k in range(len(ysides))])
    chain = with_rows(chain_ref[0], [chain_ref[1 + k] for k in range(len(ysides))])
    edge = jnp.where(odd_g, tile_index == tile_count - 1, tile_index == 0)
    chain = jnp.where(edge, 0.0, chain)
    below = jnp.where(odd_g, pair, chain)
    above = jnp.where(odd_g, chain, pair)
    ext = jnp.concatenate([below, core, above, jnp.zeros((2, 16, 128), F32)], axis=0)
    ext = ext.reshape(26 * 16, 128)
    moved = jnp.where(iota(ext.shape, 1) < 127, pltpu.roll(ext, 127, 1), 0.0)
    ext_ref[0] = ext.astype(BF16).reshape(26, 16, 128)
    ext_ref[1] = moved.astype(BF16).reshape(26, 16, 128)

    row, lane = iota((160, 128), 0), iota((160, 128), 1)
    select = jnp.where(lane == 2 * (row % 80) - 2 + 2 * (row // 80), 1.0, 0.0).astype(BF16)
    for z in range(0, 22, 2):
        around = jnp.concatenate(
            [ext_ref[m, z + d : z + d + 4].reshape(64, 128) for d in range(2) for m in range(2)],
            axis=0,
        )
        u = dot_t(select, around).astype(BF16)
        for d in range(2):
            for m in range(2):
                u_ref[z + d, :, 128 * m : 128 * (m + 1)] = u[
                    80 * m : 80 * (m + 1), 128 * d : 128 * (d + 1)
                ]

    edge_rows, edge_lanes = iota((8, 128), 0), iota((8, 128), 1)
    keep_first = (edge_rows > 0) | (edge_lanes >= 64)
    keep_last = (edge_rows < 1) & (edge_lanes < 64)

    def first_step(k, carry):
        lhs = u_ref[...].reshape(1760, 256)
        for yp in range(7):
            res = jnp.maximum(dot(lhs, w1_ref[:, 256 * yp : 256 * (yp + 1)]), 0.0)
            for d in range(22):
                for yy in range(2):
                    tile = res[80 * d : 80 * d + 72, 128 * yy : 128 * (yy + 1)]
                    head = jnp.where(keep_first, tile[:8], 0.0)
                    tail = jnp.where(keep_last, tile[64:], 0.0)
                    tile = jnp.concatenate([head, tile[8:64], tail], axis=0)
                    a_ref[d, yy, yp, :, 0:128] = tile[:64].astype(BF16)
                    after = pltpu.roll(tile, 71, 0)[:64]
                    a_ref[d, yy, yp, :, 128:256] = after.astype(BF16)
        return carry

    lax.fori_loop(0, once, first_step, 0)

    lower_half = iota((64, 128), 1) < 64

    def finish(z, act):
        act = jnp.maximum(act, 0.0).astype(BF16).reshape(6, 64, 256)
        s_ref[z] = act[1:5]
        full = act.astype(F32)
        both = full[:, :, :128] + full[:, :, 128:]
        for j in range(3):
            even, odd = both[2 * j], both[2 * j + 1]
            even = even + pltpu.roll(even, 64, 1)
            odd = odd + pltpu.roll(odd, 64, 1)
            q_ref[z, j] = jnp.where(lower_half, even, odd)

    def second_step(k, carry):
        for p in range(10):
            z = 2 * p
            products = []
            for w, (i, j) in enumerate(((0, 2), (1, 2), (2, 1), (1, 3))):
                first, second = a_ref[z + i], a_ref[z + j]
                mixed = first + second if w == 1 else first - second
                product = None
                for y in range(4):
                    lhs = mixed[y % 2, y // 2 : y // 2 + 6].reshape(384, 256)
                    at = 256 * (4 * w + y)
                    term = dot(lhs, w2_ref[at : at + 256, :])
                    product = term if product is None else product + term
                products.append(product)
            m0, m1, m2, m3 = products
            finish(z, m0 + m1 + m2)
            finish(z + 1, m1 - m2 - m3)
        return carry

    second_step(0, 0)

    for z in range(2, 18, 4):
        logits = None
        for yp in range(4):
            term = dot_t(wh_ref[48 * yp : 48 * (yp + 1), :], s_ref[z : z + 4, yp].reshape(256, 256))
            logits = term if logits is None else logits + term
        for d, plane in enumerate(side_by_side(logits)):
            fine_ref[z - 2 + d] = plane

    for copy in copies:
        copy.wait()
    slots = counts_ref.shape[2]
    total = jnp.int32(0)
    anchors = [jnp.int32(0)] * MOST
    for s in range(slots):
        dense = counts_ref[0, 0, s] >= MINC
        for j in range(MOST):
            anchors[j] = jnp.where(dense & (total == j), offsets_ref[0, 0, s], anchors[j])
        total = total + dense.astype(jnp.int32)

    rows64 = iota((64, 128), 0)
    for j in range(MOST):
        for k in range(6):
            for m in range(3):
                z = anchors[j] + 2 * k
                mean = (q_ref[z, m] + q_ref[z + 1, m]) * 0.125
                before = jnp.where(rows64 == 0, 0.0, pltpu.roll(mean, 1, 0))
                after = jnp.where(rows64 == 63, 0.0, pltpu.roll(mean, 63, 0))
                for dx, value in enumerate((before, mean, after)):
                    at = 384 * dx + 128 * m
                    lc_ref[j, k, :, at : at + 128] = value.astype(BF16)

    coarse = None
    for dz in range(3):
        lhs = lc_ref[:, dz : dz + 4].reshape(MOST * 256, 1152)
        term = dot(lhs, wc_ref[1152 * dz : 1152 * (dz + 1), :])
        coarse = term if coarse is None else coarse + term
    coarse = jnp.maximum(coarse, 0.0).astype(BF16)
    for j in range(MOST):
        logits = dot_t(wh_ref[192:240, :], coarse[256 * j : 256 * (j + 1)])
        for k, plane in enumerate(side_by_side(logits)):
            up_ref[j, k] = plane

    row, lane = iota((128, 128), 0), iota((128, 128), 1)
    order = jnp.where(lane == 2 * (row % 64) + row // 64, 1.0, 0.0).astype(BF16)
    preds = []
    for j in range(MOST):
        for u in range(CORE):
            logits = fine_ref[anchors[j] + u] + up_ref[j, u // 2]
            preds.append(jax.nn.sigmoid(logits))
    ordered = dot(jnp.concatenate(preds, axis=0).astype(BF16), order)
    pred_ref[...] = ordered.reshape(MOST, CORE, 3, 8, 128)

    for z in range(16):
        cover = jnp.float32(0.0)
        value = jnp.zeros((3, 8, 128), F32)
        for j in range(MOST):
            u = z - anchors[j]
            uf = u.astype(F32)
            tent = (uf + 1.0) * (CORE - uf) / 20.0
            inside = (j < total) & (u >= 0) & (u < CORE)
            tent = jnp.where(inside, tent, 0.0)
            cover = cover + tent
            value = value + pred_ref[j, jnp.clip(u, 0, CORE - 1)] * tent
        value = value / jnp.maximum(jnp.full((8, 128), cover, F32), 1.0)
        for c in range(3):
            out_ref[c, z] = value[c]


def neighbour_pairs(count, first):
    pairs = []
    for i in range(first, count - 1, 2):
        pairs += [(i, i + 1), (i + 1, i)]
    return pairs


def chain_pairs(tile_count, halo_count):
    def device(tile, h):
        return (tile // 2 * halo_count + h) * 2 + tile % 2

    pairs = []
    for h in range(halo_count):
        pairs += [(device(a, h), device(b, h)) for a, b in neighbour_pairs(tile_count, 1)]
        pairs += [(device(end, h), device(end, h ^ 1)) for end in (0, tile_count - 1)]
    return pairs


def local(raw_volume, tissue_counts, patch_core_offsets, w_first, w_second, w_coarse, w_head):
    halo_count = lax.axis_size("halo")
    tile_count = lax.axis_size("blocks") * lax.axis_size("gz")
    vmem = pl.BlockSpec(memory_space=pltpu.VMEM)
    hbm = pl.BlockSpec(memory_space=HBM)

    ysides = [lax.ppermute(raw_volume, "halo", neighbour_pairs(halo_count, 0))]
    if halo_count > 2:
        ysides.append(lax.ppermute(raw_volume, "halo", neighbour_pairs(halo_count, 1)))

    first_taps = jnp.transpose(w_first, (1, 2, 3, 4, 0))
    held = [first_taps, w_coarse, w_head, raw_volume]
    sources = [first_taps, w_second, w_coarse, w_head, raw_volume]
    w2, first, coarse, head, raw = pl.pallas_call(
        prepare_second,
        out_shape=[jax.ShapeDtypeStruct((4096, 256), BF16)]
        + [jax.ShapeDtypeStruct(x.shape, BF16) for x in held],
        in_specs=[hbm] * 5,
        out_specs=[vmem] * 5,
        scratch_shapes=[
            pltpu.VMEM((27 * 64, 128), F32),
            pltpu.VMEM(w_second.shape, BF16),
            pltpu.SemaphoreType.DMA((5,)),
        ],
        compiler_params=pltpu.CompilerParams(vmem_limit_bytes=24 << 20),
        cost_estimate=pl.CostEstimate(flops=1 << 20, bytes_accessed=8 << 20, transcendentals=0),
    )(*(pltpu.with_memory_space_constraint(x, HBM) for x in sources))

    stack = jnp.stack([raw] + ysides)
    odd = lax.axis_index("gz") == 1
    first_layers, last_layers = stack[:, :MARGIN], stack[:, -MARGIN:]
    pair = lax.ppermute(jnp.where(odd, first_layers, last_layers), "gz", [(0, 1), (1, 0)])
    chain = lax.ppermute(
        jnp.where(odd, last_layers, first_layers),
        ("blocks", "halo", "gz"),
        chain_pairs(tile_count, halo_count),
    )

    w1, wc, wh = pl.pallas_call(
        prepare_rest,
        out_shape=[
            jax.ShapeDtypeStruct((256, 1792), BF16),
            jax.ShapeDtypeStruct((3456, 256), BF16),
            jax.ShapeDtypeStruct((240, 256), BF16),
        ],
        in_specs=[vmem] * 3,
        out_specs=[vmem] * 3,
        scratch_shapes=[pltpu.VMEM((27 * 64, 128), F32)],
        compiler_params=pltpu.CompilerParams(vmem_limit_bytes=16 << 20),
        cost_estimate=pl.CostEstimate(flops=1 << 20, bytes_accessed=6 << 20, transcendentals=0),
    )(first, coarse, head)

    def body(*refs):
        tile_kernel(halo_count, tile_count, *refs)

    return pl.pallas_call(
        body,
        out_shape=jax.ShapeDtypeStruct((3, 16, 8, 128), F32),
        in_specs=[hbm, hbm] + [vmem] * (7 + len(ysides)),
        out_specs=vmem,
        scratch_shapes=[
            pltpu.VMEM((2, 26, 16, 128), BF16),
            pltpu.VMEM((22, 80, 256), BF16),
            pltpu.VMEM((22, 2, 7, 64, 256), BF16),
            pltpu.VMEM((20, 4, 64, 256), BF16),
            pltpu.VMEM((20, 3, 64, 128), F32),
            pltpu.VMEM((MOST, 6, 64, 1152), BF16),
            pltpu.VMEM((16, 24, 128), F32),
            pltpu.VMEM((MOST, 4, 24, 128), F32),
            pltpu.VMEM((MOST, CORE, 3, 8, 128), F32),
            pltpu.SMEM(tissue_counts.shape, jnp.int32),
            pltpu.SMEM(patch_core_offsets.shape, jnp.int32),
            pltpu.SemaphoreType.DMA((2,)),
        ],
        compiler_params=pltpu.CompilerParams(vmem_limit_bytes=40 << 20),
        cost_estimate=pl.CostEstimate(flops=16 << 30, bytes_accessed=5 << 20, transcendentals=0),
    )(
        pltpu.with_memory_space_constraint(tissue_counts, HBM),
        pltpu.with_memory_space_constraint(patch_core_offsets, HBM),
        raw,
        *ysides,
        pair,
        chain,
        w1,
        w2,
        wc,
        wh,
    )


def solution(mesh):
    in_specs = (
        P(("groups", "blocks", "gz"), "halo", None),
        P(("groups", "blocks", "gz"), "halo", None),
        P(("groups", "blocks", "gz"), "halo", None),
        P(),
        P(),
        P(),
        P(),
    )
    out_specs = P(None, ("groups", "blocks", "gz"), "halo", None)
    return jax.shard_map(local, mesh=mesh, in_specs=in_specs, out_specs=out_specs, check_vma=False)
```

```python
import jax
import jax.numpy as jnp
from jax import lax
from jax.experimental import pallas as pl
from jax.experimental.pallas import tpu as pltpu
from jax.sharding import PartitionSpec as P

CORE = 8
MARGIN = 4
MOST = 3
MINC = 4096
F32 = jnp.float32
BF16 = jnp.bfloat16
HBM = pltpu.HBM


def dot(a, b):
    return lax.dot_general(a, b, (((1,), (0,)), ((), ())), preferred_element_type=F32)


def dot_t(a, b):
    return lax.dot_general(a, b, (((1,), (1,)), ((), ())), preferred_element_type=F32)


def iota(shape, dim):
    return lax.broadcasted_iota(jnp.int32, shape, dim)


def tap_rows(flat_ref, rows_ref):
    taps = flat_ref.shape[0]
    for j in range(32):
        block = flat_ref[:, 128 * j : 128 * (j + 1)].astype(F32)
        rows_ref[pl.ds(2 * j, taps, stride=64), :] = block
        rows_ref[pl.ds(2 * j + 1, taps, stride=64), :] = pltpu.roll(block, 64, 1)


def band(w0, w1, w2):
    lower = iota((64, 128), 1) < 64
    d1 = jnp.concatenate([w1, w0], axis=0).T[:64]
    d2 = jnp.concatenate([w2, w1], axis=0).T[:64]
    d0 = jnp.where(lower, pltpu.roll(d1, 64, 1), 0.0)
    d3 = jnp.where(lower, 0.0, pltpu.roll(d2, 64, 1))
    return [d.astype(BF16) for d in (d0, d1, d2, d3)]


def put_bands(out_ref, start, blocks, columns):
    for i, block in enumerate(blocks):
        out_ref[start + 64 * i : start + 64 * (i + 1), columns : columns + 128] = block


def prepare_second(first_hbm, second_hbm, coarse_hbm, head_hbm, raw_hbm, *refs):
    (w2_ref, first_ref, coarse_ref, head_ref, raw_ref, rows_ref, second_ref, sems) = refs
    copies = [
        pltpu.make_async_copy(src, dst, sems.at[i])
        for i, (src, dst) in enumerate(
            (
                (second_hbm, second_ref),
                (raw_hbm, raw_ref),
                (first_hbm, first_ref),
                (head_hbm, head_ref),
                (coarse_hbm, coarse_ref),
            )
        )
    ]
    for copy in copies:
        copy.start()

    zeros = jnp.zeros((256, 128), BF16)
    for w in range(4):
        w2_ref[1024 * w : 1024 * w + 256, 128:256] = zeros
        w2_ref[1024 * w + 768 : 1024 * w + 1024, 0:128] = zeros
    copies[0].wait()
    tap_rows(second_ref, rows_ref)
    for w in range(4):
        for dy in range(3):
            taps = []
            for dx in range(3):
                g0, g1, g2 = (
                    rows_ref[64 * t : 64 * (t + 1), :] for t in range(3 * dy + dx, 27, 9)
                )
                taps.append((g0, 0.5 * (g0 + g1 + g2), 0.5 * (g0 - g1 + g2), g2)[w])
            blocks = band(*taps)
            for yy in range(2):
                put_bands(w2_ref, 256 * (4 * w + dy + yy), blocks, 128 * yy)
    for copy in copies[1:]:
        copy.wait()


def prepare_rest(first_ref, coarse_ref, head_ref, w1_ref, wc_ref, wh_ref, rows_ref):
    shape = (256, 27)
    row, lane = iota(shape, 0), iota(shape, 1)
    xo, dz, y = row // 64, (row // 16) % 4, row % 16
    first = jnp.concatenate(
        [first_ref[0, k // 3, k % 3].astype(F32) for k in range(9)], axis=0
    ).astype(BF16)
    parts = []
    for yy in range(2):
        for xx in range(2):
            dy, dx = y - yy, xo - xx
            valid = (dz < 3) & (dy >= 0) & (dy < 3) & (dx >= 0) & (dx < 3)
            pick = jnp.where(valid & (lane == dz * 9 + dy * 3 + dx), 1.0, 0.0).astype(BF16)
            parts.append(dot(pick, first))
    base = jnp.concatenate(parts, axis=1)
    for yp in range(7):
        moved = base if yp == 0 else pltpu.roll(base, 2 * yp, 0)
        w1_ref[:, 256 * yp : 256 * (yp + 1)] = moved.astype(BF16)

    wide = (240, 256)
    row, lane = iota(wide, 0), iota(wide, 1)
    yp, xx, y = row // 48, (row // 24) % 2, row % 8
    o = (row // 8) % 3
    head = head_ref[...].astype(F32)
    tiled = jnp.concatenate([head] * 4, axis=1)
    value = jnp.where(o == 0, tiled[0:1], jnp.where(o == 1, tiled[1:2], tiled[2:3]))
    fine = (y // 2 == yp) & (y % 2 == lane // 128) & (xx == (lane // 64) % 2)
    up = (yp == 4) & (y // 2 == lane // 64)
    wh_ref[...] = jnp.where(fine | up, value, 0.0).astype(BF16)

    tap_rows(coarse_ref, rows_ref)
    zeros = jnp.zeros((128, 128), BF16)
    for dz in range(3):
        for dx in range(3):
            blocks = band(
                *(rows_ref[64 * t : 64 * (t + 1), :] for t in range(9 * dz + dx, 9 * dz + 9, 3))
            )
            start = 384 * (3 * dz + dx)
            for half in range(2):
                put_bands(wc_ref, start + 128 * half, blocks, 128 * half)
            wc_ref[start + 256 : start + 384, 0:128] = zeros
            wc_ref[start : start + 128, 128:256] = zeros


def side_by_side(logits):
    lower = iota((24, 128), 1) < 64
    planes = []
    for half in range(2):
        tile = logits[:, 128 * half : 128 * (half + 1)]
        even, odd = tile[:24], tile[24:]
        planes.append(jnp.where(lower, even, pltpu.roll(odd, 64, 1)))
        planes.append(jnp.where(lower, pltpu.roll(even, 64, 1), odd))
    return planes


def tile_kernel(halo_count, tile_count, counts_hbm, offsets_hbm, raw_ref, *refs):
    ysides = refs[: 1 + (halo_count > 2)]
    refs = refs[len(ysides) :]
    (pair_ref, chain_ref, w1_ref, w2_ref, wc_ref, wh_ref, out_ref) = refs[:7]
    (ext_ref, u_ref, a_ref, s_ref, q_ref, lc_ref, fine_ref, up_ref, pred_ref) = refs[7:16]
    counts_ref, offsets_ref, sems = refs[16:]
    copies = [
        pltpu.make_async_copy(counts_hbm, counts_ref, sems.at[0]),
        pltpu.make_async_copy(offsets_hbm, offsets_ref, sems.at[1]),
    ]
    for copy in copies:
        copy.start()

    halo_index = lax.axis_index("halo")
    gz_index = lax.axis_index("gz")
    tile_index = lax.axis_index("blocks") * 2 + gz_index

    odd_h = halo_index % 2 == 1
    odd_g = gz_index == 1
    once = jnp.minimum(tile_index + 1, 1)

    def with_rows(own, sides):
        own = own.astype(F32)
        near = sides[0].astype(F32)
        far = sides[1].astype(F32) if len(sides) > 1 else jnp.zeros_like(near)
        below = jnp.where(odd_h, near, far)
        above = jnp.where(odd_h, far, near)
        return jnp.concatenate([below[:, 4:8], own, above[:, 0:4]], axis=1)

    core = with_rows(raw_ref[...], [r[...] for r in ysides])
    pair = with_rows(pair_ref[0], [pair_ref[1 + k] for k in range(len(ysides))])
    chain = with_rows(chain_ref[0], [chain_ref[1 + k] for k in range(len(ysides))])
    edge = jnp.where(odd_g, tile_index == tile_count - 1, tile_index == 0)
    chain = jnp.where(edge, 0.0, chain)
    below = jnp.where(odd_g, pair, chain)
    above = jnp.where(odd_g, chain, pair)
    ext = jnp.concatenate([below, core, above, jnp.zeros((2, 16, 128), F32)], axis=0)
    ext = ext.reshape(26 * 16, 128)
    moved = jnp.where(iota(ext.shape, 1) < 127, pltpu.roll(ext, 127, 1), 0.0)
    ext_ref[0] = ext.astype(BF16).reshape(26, 16, 128)
    ext_ref[1] = moved.astype(BF16).reshape(26, 16, 128)

    row, lane = iota((160, 128), 0), iota((160, 128), 1)
    select = jnp.where(lane == 2 * (row % 80) - 2 + 2 * (row // 80), 1.0, 0.0).astype(BF16)
    for z in range(0, 22, 2):
        around = jnp.concatenate(
            [ext_ref[m, z + d : z + d + 4].reshape(64, 128) for d in range(2) for m in range(2)],
            axis=0,
        )
        u = dot_t(select, around).astype(BF16)
        for d in range(2):
            for m in range(2):
                u_ref[z + d, :, 128 * m : 128 * (m + 1)] = u[
                    80 * m : 80 * (m + 1), 128 * d : 128 * (d + 1)
                ]

    edge_rows, edge_lanes = iota((8, 128), 0), iota((8, 128), 1)
    keep_first = (edge_rows > 0) | (edge_lanes >= 64)
    keep_last = (edge_rows < 1) & (edge_lanes < 64)

    def first_step(k, carry):
        lhs = u_ref[...].reshape(1760, 256)
        for yp in range(7):
            res = jnp.maximum(dot(lhs, w1_ref[:, 256 * yp : 256 * (yp + 1)]), 0.0)
            for d in range(22):
                for yy in range(2):
                    tile = res[80 * d : 80 * d + 72, 128 * yy : 128 * (yy + 1)]
                    head = jnp.where(keep_first, tile[:8], 0.0)
                    tail = jnp.where(keep_last, tile[64:], 0.0)
                    tile = jnp.concatenate([head, tile[8:64], tail], axis=0)
                    a_ref[d, yy, yp, :, 0:128] = tile[:64].astype(BF16)
                    after = pltpu.roll(tile, 71, 0)[:64]
                    a_ref[d, yy, yp, :, 128:256] = after.astype(BF16)
        return carry

    lax.fori_loop(0, once, first_step, 0)

    for copy in copies:
        copy.wait()
    slots = counts_ref.shape[2]
    total = jnp.int32(0)
    anchors = [jnp.int32(0)] * MOST
    for s in range(slots):
        dense = counts_ref[0, 0, s] >= MINC
        for j in range(MOST):
            anchors[j] = jnp.where(dense & (total == j), offsets_ref[0, 0, s], anchors[j])
        total = total + dense.astype(jnp.int32)

    lower_half = iota((64, 128), 1) < 64

    def finish(z, act):
        act = jnp.maximum(act, 0.0).astype(BF16).reshape(6, 64, 256)
        s_ref[z] = act[1:5]
        full = act.astype(F32)
        both = full[:, :, :128] + full[:, :, 128:]
        for j in range(3):
            even, odd = both[2 * j], both[2 * j + 1]
            even = even + pltpu.roll(even, 64, 1)
            odd = odd + pltpu.roll(odd, 64, 1)
            q_ref[z, j] = jnp.where(lower_half, even, odd)

    def second_step(k, carry):
        for p in range(10):
            z = 2 * p
            products = []
            for w, (i, j) in enumerate(((0, 2), (1, 2), (2, 1), (1, 3))):
                first, second = a_ref[z + i], a_ref[z + j]
                mixed = first + second if w == 1 else first - second
                product = None
                for y in range(4):
                    lhs = mixed[y % 2, y // 2 : y // 2 + 6].reshape(384, 256)
                    at = 256 * (4 * w + y)
                    term = dot(lhs, w2_ref[at : at + 256, :])
                    product = term if product is None else product + term
                products.append(product)
            m0, m1, m2, m3 = products
            finish(z, m0 + m1 + m2)
            finish(z + 1, m1 - m2 - m3)
        return carry

    second_step(0, 0)

    for z in range(2, 18, 4):
        logits = None
        for yp in range(4):
            term = dot_t(wh_ref[48 * yp : 48 * (yp + 1), :], s_ref[z : z + 4, yp].reshape(256, 256))
            logits = term if logits is None else logits + term
        for d, plane in enumerate(side_by_side(logits)):
            fine_ref[z - 2 + d] = plane

    rows64 = iota((64, 128), 0)
    for j in range(MOST):
        for k in range(6):
            for m in range(3):
                z = anchors[j] + 2 * k
                mean = (q_ref[z, m] + q_ref[z + 1, m]) * 0.125
                before = jnp.where(rows64 == 0, 0.0, pltpu.roll(mean, 1, 0))
                after = jnp.where(rows64 == 63, 0.0, pltpu.roll(mean, 63, 0))
                for dx, value in enumerate((before, mean, after)):
                    at = 384 * dx + 128 * m
                    lc_ref[j, k, :, at : at + 128] = value.astype(BF16)

    coarse = None
    for dz in range(3):
        lhs = lc_ref[:, dz : dz + 4].reshape(MOST * 256, 1152)
        term = dot(lhs, wc_ref[1152 * dz : 1152 * (dz + 1), :])
        coarse = term if coarse is None else coarse + term
    coarse = jnp.maximum(coarse, 0.0).astype(BF16)
    for j in range(MOST):
        logits = dot_t(wh_ref[192:240, :], coarse[256 * j : 256 * (j + 1)])
        for k, plane in enumerate(side_by_side(logits)):
            up_ref[j, k] = plane

    row, lane = iota((128, 128), 0), iota((128, 128), 1)
    order = jnp.where(lane == 2 * (row % 64) + row // 64, 1.0, 0.0).astype(BF16)
    preds = []
    for j in range(MOST):
        for u in range(CORE):
            logits = fine_ref[anchors[j] + u] + up_ref[j, u // 2]
            preds.append(jax.nn.sigmoid(logits))
    ordered = dot(jnp.concatenate(preds, axis=0).astype(BF16), order)
    pred_ref[...] = ordered.reshape(MOST, CORE, 3, 8, 128)

    for z in range(16):
        cover = jnp.float32(0.0)
        value = jnp.zeros((3, 8, 128), F32)
        for j in range(MOST):
            u = z - anchors[j]
            uf = u.astype(F32)
            tent = (uf + 1.0) * (CORE - uf) / 20.0
            inside = (j < total) & (u >= 0) & (u < CORE)
            tent = jnp.where(inside, tent, 0.0)
            cover = cover + tent
            value = value + pred_ref[j, jnp.clip(u, 0, CORE - 1)] * tent
        value = value / jnp.maximum(jnp.full((8, 128), cover, F32), 1.0)
        for c in range(3):
            out_ref[c, z] = value[c]


def neighbour_pairs(count, first):
    pairs = []
    for i in range(first, count - 1, 2):
        pairs += [(i, i + 1), (i + 1, i)]
    return pairs


def chain_pairs(tile_count, halo_count):
    def device(tile, h):
        return (tile // 2 * halo_count + h) * 2 + tile % 2

    pairs = []
    for h in range(halo_count):
        pairs += [(device(a, h), device(b, h)) for a, b in neighbour_pairs(tile_count, 1)]
        pairs += [(device(end, h), device(end, h ^ 1)) for end in (0, tile_count - 1)]
    return pairs


def local(raw_volume, tissue_counts, patch_core_offsets, w_first, w_second, w_coarse, w_head):
    halo_count = lax.axis_size("halo")
    tile_count = lax.axis_size("blocks") * lax.axis_size("gz")
    vmem = pl.BlockSpec(memory_space=pltpu.VMEM)
    hbm = pl.BlockSpec(memory_space=HBM)

    ysides = [lax.ppermute(raw_volume, "halo", neighbour_pairs(halo_count, 0))]
    if halo_count > 2:
        ysides.append(lax.ppermute(raw_volume, "halo", neighbour_pairs(halo_count, 1)))

    first_taps = jnp.transpose(w_first, (1, 2, 3, 4, 0))
    held = [first_taps, w_coarse, w_head, raw_volume]
    sources = [first_taps, w_second, w_coarse, w_head, raw_volume]
    w2, first, coarse, head, raw = pl.pallas_call(
        prepare_second,
        out_shape=[jax.ShapeDtypeStruct((4096, 256), BF16)]
        + [jax.ShapeDtypeStruct(x.shape, BF16) for x in held],
        in_specs=[hbm] * 5,
        out_specs=[vmem] * 5,
        scratch_shapes=[
            pltpu.VMEM((27 * 64, 128), F32),
            pltpu.VMEM(w_second.shape, BF16),
            pltpu.SemaphoreType.DMA((5,)),
        ],
        compiler_params=pltpu.CompilerParams(vmem_limit_bytes=24 << 20),
        cost_estimate=pl.CostEstimate(flops=1 << 20, bytes_accessed=8 << 20, transcendentals=0),
    )(*(pltpu.with_memory_space_constraint(x, HBM) for x in sources))

    stack = jnp.stack([raw] + ysides)
    odd = lax.axis_index("gz") == 1
    first_layers, last_layers = stack[:, :MARGIN], stack[:, -MARGIN:]
    pair = lax.ppermute(jnp.where(odd, first_layers, last_layers), "gz", [(0, 1), (1, 0)])
    chain = lax.ppermute(
        jnp.where(odd, last_layers, first_layers),
        ("blocks", "halo", "gz"),
        chain_pairs(tile_count, halo_count),
    )

    w1, wc, wh = pl.pallas_call(
        prepare_rest,
        out_shape=[
            jax.ShapeDtypeStruct((256, 1792), BF16),
            jax.ShapeDtypeStruct((3456, 256), BF16),
            jax.ShapeDtypeStruct((240, 256), BF16),
        ],
        in_specs=[vmem] * 3,
        out_specs=[vmem] * 3,
        scratch_shapes=[pltpu.VMEM((27 * 64, 128), F32)],
        compiler_params=pltpu.CompilerParams(vmem_limit_bytes=16 << 20),
        cost_estimate=pl.CostEstimate(flops=1 << 20, bytes_accessed=6 << 20, transcendentals=0),
    )(first, coarse, head)

    def body(*refs):
        tile_kernel(halo_count, tile_count, *refs)

    return pl.pallas_call(
        body,
        out_shape=jax.ShapeDtypeStruct((3, 16, 8, 128), F32),
        in_specs=[hbm, hbm] + [vmem] * (7 + len(ysides)),
        out_specs=vmem,
        scratch_shapes=[
            pltpu.VMEM((2, 26, 16, 128), BF16),
            pltpu.VMEM((22, 80, 256), BF16),
            pltpu.VMEM((22, 2, 7, 64, 256), BF16),
            pltpu.VMEM((20, 4, 64, 256), BF16),
            pltpu.VMEM((20, 3, 64, 128), F32),
            pltpu.VMEM((MOST, 6, 64, 1152), BF16),
            pltpu.VMEM((16, 24, 128), F32),
            pltpu.VMEM((MOST, 4, 24, 128), F32),
            pltpu.VMEM((MOST, CORE, 3, 8, 128), F32),
            pltpu.SMEM(tissue_counts.shape, jnp.int32),
            pltpu.SMEM(patch_core_offsets.shape, jnp.int32),
            pltpu.SemaphoreType.DMA((2,)),
        ],
        compiler_params=pltpu.CompilerParams(vmem_limit_bytes=40 << 20),
        cost_estimate=pl.CostEstimate(flops=16 << 30, bytes_accessed=5 << 20, transcendentals=0),
    )(
        pltpu.with_memory_space_constraint(tissue_counts, HBM),
        pltpu.with_memory_space_constraint(patch_core_offsets, HBM),
        raw,
        *ysides,
        pair,
        chain,
        w1,
        w2,
        wc,
        wh,
    )


def solution(mesh):
    in_specs = (
        P(("groups", "blocks", "gz"), "halo", None),
        P(("groups", "blocks", "gz"), "halo", None),
        P(("groups", "blocks", "gz"), "halo", None),
        P(),
        P(),
        P(),
        P(),
    )
    out_specs = P(None, ("groups", "blocks", "gz"), "halo", None)
    return jax.shard_map(local, mesh=mesh, in_specs=in_specs, out_specs=out_specs, check_vma=False)
```

```python
import jax
import jax.numpy as jnp
from jax import lax
from jax.experimental import pallas as pl
from jax.experimental.pallas import tpu as pltpu
from jax.sharding import PartitionSpec as P

CORE = 8
MARGIN = 4
MOST = 3
MINC = 4096
F32 = jnp.float32
BF16 = jnp.bfloat16
HBM = pltpu.HBM


def dot(a, b):
    return lax.dot_general(a, b, (((1,), (0,)), ((), ())), preferred_element_type=F32)


def dot_t(a, b):
    return lax.dot_general(a, b, (((1,), (1,)), ((), ())), preferred_element_type=F32)


def iota(shape, dim):
    return lax.broadcasted_iota(jnp.int32, shape, dim)


def tap_rows(flat_ref, rows_ref):
    taps = flat_ref.shape[0]
    for j in range(32):
        block = flat_ref[:, 128 * j : 128 * (j + 1)].astype(F32)
        rows_ref[pl.ds(2 * j, taps, stride=64), :] = block
        rows_ref[pl.ds(2 * j + 1, taps, stride=64), :] = pltpu.roll(block, 64, 1)


def band(w0, w1, w2):
    lower = iota((64, 128), 1) < 64
    d1 = jnp.concatenate([w1, w0], axis=0).T[:64]
    d2 = jnp.concatenate([w2, w1], axis=0).T[:64]
    d0 = jnp.where(lower, pltpu.roll(d1, 64, 1), 0.0)
    d3 = jnp.where(lower, 0.0, pltpu.roll(d2, 64, 1))
    return [d.astype(BF16) for d in (d0, d1, d2, d3)]


def put_bands(out_ref, start, blocks, columns):
    for i, block in enumerate(blocks):
        out_ref[start + 64 * i : start + 64 * (i + 1), columns : columns + 128] = block


def prepare_second(first_hbm, second_hbm, coarse_hbm, head_hbm, raw_hbm, *refs):
    (w2_ref, first_ref, coarse_ref, head_ref, raw_ref, rows_ref, second_ref, sems) = refs
    copies = [
        pltpu.make_async_copy(src, dst, sems.at[i])
        for i, (src, dst) in enumerate(
            (
                (second_hbm, second_ref),
                (raw_hbm, raw_ref),
                (first_hbm, first_ref),
                (head_hbm, head_ref),
                (coarse_hbm, coarse_ref),
            )
        )
    ]
    for copy in copies:
        copy.start()

    zeros = jnp.zeros((256, 128), BF16)
    for w in range(4):
        w2_ref[1024 * w : 1024 * w + 256, 128:256] = zeros
        w2_ref[1024 * w + 768 : 1024 * w + 1024, 0:128] = zeros
    copies[0].wait()
    tap_rows(second_ref, rows_ref)
    for w in range(4):
        for dy in range(3):
            taps = []
            for dx in range(3):
                g0, g1, g2 = (
                    rows_ref[64 * t : 64 * (t + 1), :] for t in range(3 * dy + dx, 27, 9)
                )
                taps.append((g0, 0.5 * (g0 + g1 + g2), 0.5 * (g0 - g1 + g2), g2)[w])
            blocks = band(*taps)
            for yy in range(2):
                put_bands(w2_ref, 256 * (4 * w + dy + yy), blocks, 128 * yy)
    for copy in copies[1:]:
        copy.wait()


def prepare_rest(first_ref, coarse_ref, head_ref, w1_ref, wc_ref, wh_ref, rows_ref):
    shape = (256, 27)
    row, lane = iota(shape, 0), iota(shape, 1)
    xo, dz, y = row // 64, (row // 16) % 4, row % 16
    first = jnp.concatenate(
        [first_ref[0, k // 3, k % 3].astype(F32) for k in range(9)], axis=0
    ).astype(BF16)
    parts = []
    for yy in range(2):
        for xx in range(2):
            dy, dx = y - yy, xo - xx
            valid = (dz < 3) & (dy >= 0) & (dy < 3) & (dx >= 0) & (dx < 3)
            pick = jnp.where(valid & (lane == dz * 9 + dy * 3 + dx), 1.0, 0.0).astype(BF16)
            parts.append(dot(pick, first))
    base = jnp.concatenate(parts, axis=1)
    for yp in range(7):
        moved = base if yp == 0 else pltpu.roll(base, 2 * yp, 0)
        w1_ref[:, 256 * yp : 256 * (yp + 1)] = moved.astype(BF16)

    wide = (240, 256)
    row, lane = iota(wide, 0), iota(wide, 1)
    yp, xx, y = row // 48, (row // 24) % 2, row % 8
    o = (row // 8) % 3
    head = head_ref[...].astype(F32)
    tiled = jnp.concatenate([head] * 4, axis=1)
    value = jnp.where(o == 0, tiled[0:1], jnp.where(o == 1, tiled[1:2], tiled[2:3]))
    fine = (y // 2 == yp) & (y % 2 == lane // 128) & (xx == (lane // 64) % 2)
    up = (yp == 4) & (y // 2 == lane // 64)
    wh_ref[...] = jnp.where(fine | up, value, 0.0).astype(BF16)

    tap_rows(coarse_ref, rows_ref)
    zeros = jnp.zeros((128, 128), BF16)
    for dz in range(3):
        for dx in range(3):
            blocks = band(
                *(rows_ref[64 * t : 64 * (t + 1), :] for t in range(9 * dz + dx, 9 * dz + 9, 3))
            )
            start = 384 * (3 * dz + dx)
            for half in range(2):
                put_bands(wc_ref, start + 128 * half, blocks, 128 * half)
            wc_ref[start + 256 : start + 384, 0:128] = zeros
            wc_ref[start : start + 128, 128:256] = zeros


def side_by_side(logits):
    lower = iota((24, 128), 1) < 64
    planes = []
    for half in range(2):
        tile = logits[:, 128 * half : 128 * (half + 1)]
        even, odd = tile[:24], tile[24:]
        planes.append(jnp.where(lower, even, pltpu.roll(odd, 64, 1)))
        planes.append(jnp.where(lower, pltpu.roll(even, 64, 1), odd))
    return planes


def tile_kernel(halo_count, tile_count, counts_hbm, offsets_hbm, raw_ref, *refs):
    ysides = refs[: 1 + (halo_count > 2)]
    refs = refs[len(ysides) :]
    (pair_ref, chain_ref, w1_ref, w2_ref, wc_ref, wh_ref, out_ref) = refs[:7]
    (ext_ref, u_ref, a_ref, s_ref, q_ref, lc_ref, fine_ref, up_ref, pred_ref) = refs[7:16]
    counts_ref, offsets_ref, sems = refs[16:]
    copies = [
        pltpu.make_async_copy(counts_hbm, counts_ref, sems.at[0]),
        pltpu.make_async_copy(offsets_hbm, offsets_ref, sems.at[1]),
    ]
    for copy in copies:
        copy.start()

    halo_index = lax.axis_index("halo")
    gz_index = lax.axis_index("gz")
    tile_index = lax.axis_index("blocks") * 2 + gz_index

    odd_h = halo_index % 2 == 1
    odd_g = gz_index == 1
    once = jnp.minimum(tile_index + 1, 1)

    def with_rows(own, sides):
        own = own.astype(F32)
        near = sides[0].astype(F32)
        far = sides[1].astype(F32) if len(sides) > 1 else jnp.zeros_like(near)
        below = jnp.where(odd_h, near, far)
        above = jnp.where(odd_h, far, near)
        return jnp.concatenate([below[:, 4:8], own, above[:, 0:4]], axis=1)

    core = with_rows(raw_ref[...], [r[...] for r in ysides])
    pair = with_rows(pair_ref[0], [pair_ref[1 + k] for k in range(len(ysides))])
    chain = with_rows(chain_ref[0], [chain_ref[1 + k] for k in range(len(ysides))])
    edge = jnp.where(odd_g, tile_index == tile_count - 1, tile_index == 0)
    chain = jnp.where(edge, 0.0, chain)
    below = jnp.where(odd_g, pair, chain)
    above = jnp.where(odd_g, chain, pair)
    ext = jnp.concatenate([below, core, above, jnp.zeros((2, 16, 128), F32)], axis=0)
    ext = ext.reshape(26 * 16, 128)
    moved = jnp.where(iota(ext.shape, 1) < 127, pltpu.roll(ext, 127, 1), 0.0)
    ext_ref[0] = ext.astype(BF16).reshape(26, 16, 128)
    ext_ref[1] = moved.astype(BF16).reshape(26, 16, 128)

    row, lane = iota((160, 128), 0), iota((160, 128), 1)
    select = jnp.where(lane == 2 * (row % 80) - 2 + 2 * (row // 80), 1.0, 0.0).astype(BF16)
    for z in range(0, 22, 2):
        around = jnp.concatenate(
            [ext_ref[m, z + d : z + d + 4].reshape(64, 128) for d in range(2) for m in range(2)],
            axis=0,
        )
        u = dot_t(select, around).astype(BF16)
        for d in range(2):
            for m in range(2):
                u_ref[z + d, :, 128 * m : 128 * (m + 1)] = u[
                    80 * m : 80 * (m + 1), 128 * d : 128 * (d + 1)
                ]

    edge_rows, edge_lanes = iota((8, 128), 0), iota((8, 128), 1)
    keep_first = (edge_rows > 0) | (edge_lanes >= 64)
    keep_last = (edge_rows < 1) & (edge_lanes < 64)

    def first_step(k, carry):
        lhs = u_ref[...].reshape(1760, 256)
        for yp in range(7):
            res = jnp.maximum(dot(lhs, w1_ref[:, 256 * yp : 256 * (yp + 1)]), 0.0)
            for d in range(22):
                for yy in range(2):
                    tile = res[80 * d : 80 * d + 72, 128 * yy : 128 * (yy + 1)]
                    head = jnp.where(keep_first, tile[:8], 0.0)
                    tail = jnp.where(keep_last, tile[64:], 0.0)
                    tile = jnp.concatenate([head, tile[8:64], tail], axis=0)
                    a_ref[d, yy, yp, :, 0:128] = tile[:64].astype(BF16)
                    after = pltpu.roll(tile, 71, 0)[:64]
                    a_ref[d, yy, yp, :, 128:256] = after.astype(BF16)
        return carry

    lax.fori_loop(0, once, first_step, 0)

    for copy in copies:
        copy.wait()
    slots = counts_ref.shape[2]
    total = jnp.int32(0)
    anchors = [jnp.int32(0)] * MOST
    for s in range(slots):
        dense = counts_ref[0, 0, s] >= MINC
        for j in range(MOST):
            anchors[j] = jnp.where(dense & (total == j), offsets_ref[0, 0, s], anchors[j])
        total = total + dense.astype(jnp.int32)

    lower_half = iota((64, 128), 1) < 64

    def finish(z, act):
        act = jnp.maximum(act, 0.0).astype(BF16).reshape(6, 64, 256)
        s_ref[z] = act[1:5]
        full = act.astype(F32)
        both = full[:, :, :128] + full[:, :, 128:]
        for j in range(3):
            even, odd = both[2 * j], both[2 * j + 1]
            even = even + pltpu.roll(even, 64, 1)
            odd = odd + pltpu.roll(odd, 64, 1)
            q_ref[z, j] = jnp.where(lower_half, even, odd)

    def put_head(z):
        logits = None
        for yp in range(4):
            term = dot_t(wh_ref[48 * yp : 48 * (yp + 1), :], s_ref[z : z + 4, yp].reshape(256, 256))
            logits = term if logits is None else logits + term
        for d, plane in enumerate(side_by_side(logits)):
            fine_ref[z - 2 + d] = plane

    def second_step(k, carry):
        for p in range(10):
            z = 2 * p
            products = []
            for w, (i, j) in enumerate(((0, 2), (1, 2), (2, 1), (1, 3))):
                first, second = a_ref[z + i], a_ref[z + j]
                mixed = first + second if w == 1 else first - second
                product = None
                for y in range(4):
                    lhs = mixed[y % 2, y // 2 : y // 2 + 6].reshape(384, 256)
                    at = 256 * (4 * w + y)
                    term = dot(lhs, w2_ref[at : at + 256, :])
                    product = term if product is None else product + term
                products.append(product)
            m0, m1, m2, m3 = products
            finish(z, m0 + m1 + m2)
            finish(z + 1, m1 - m2 - m3)
            if p in (2, 4, 6, 8):
                put_head(z - 2)
        return carry

    second_step(0, 0)

    rows64 = iota((64, 128), 0)
    for j in range(MOST):
        for k in range(6):
            for m in range(3):
                z = anchors[j] + 2 * k
                mean = (q_ref[z, m] + q_ref[z + 1, m]) * 0.125
                before = jnp.where(rows64 == 0, 0.0, pltpu.roll(mean, 1, 0))
                after = jnp.where(rows64 == 63, 0.0, pltpu.roll(mean, 63, 0))
                for dx, value in enumerate((before, mean, after)):
                    at = 384 * dx + 128 * m
                    lc_ref[j, k, :, at : at + 128] = value.astype(BF16)

    coarse = None
    for dz in range(3):
        lhs = lc_ref[:, dz : dz + 4].reshape(MOST * 256, 1152)
        term = dot(lhs, wc_ref[1152 * dz : 1152 * (dz + 1), :])
        coarse = term if coarse is None else coarse + term
    coarse = jnp.maximum(coarse, 0.0).astype(BF16)
    for j in range(MOST):
        logits = dot_t(wh_ref[192:240, :], coarse[256 * j : 256 * (j + 1)])
        for k, plane in enumerate(side_by_side(logits)):
            up_ref[j, k] = plane

    row, lane = iota((128, 128), 0), iota((128, 128), 1)
    order = jnp.where(lane == 2 * (row % 64) + row // 64, 1.0, 0.0).astype(BF16)
    preds = []
    for j in range(MOST):
        for u in range(CORE):
            logits = fine_ref[anchors[j] + u] + up_ref[j, u // 2]
            preds.append(jax.nn.sigmoid(logits))
    ordered = dot(jnp.concatenate(preds, axis=0).astype(BF16), order)
    pred_ref[...] = ordered.reshape(MOST, CORE, 3, 8, 128)

    for z in range(16):
        cover = jnp.float32(0.0)
        value = jnp.zeros((3, 8, 128), F32)
        for j in range(MOST):
            u = z - anchors[j]
            uf = u.astype(F32)
            tent = (uf + 1.0) * (CORE - uf) / 20.0
            inside = (j < total) & (u >= 0) & (u < CORE)
            tent = jnp.where(inside, tent, 0.0)
            cover = cover + tent
            value = value + pred_ref[j, jnp.clip(u, 0, CORE - 1)] * tent
        value = value / jnp.maximum(jnp.full((8, 128), cover, F32), 1.0)
        for c in range(3):
            out_ref[c, z] = value[c]


def neighbour_pairs(count, first):
    pairs = []
    for i in range(first, count - 1, 2):
        pairs += [(i, i + 1), (i + 1, i)]
    return pairs


def chain_pairs(tile_count, halo_count):
    def device(tile, h):
        return (tile // 2 * halo_count + h) * 2 + tile % 2

    pairs = []
    for h in range(halo_count):
        pairs += [(device(a, h), device(b, h)) for a, b in neighbour_pairs(tile_count, 1)]
        pairs += [(device(end, h), device(end, h ^ 1)) for end in (0, tile_count - 1)]
    return pairs


def local(raw_volume, tissue_counts, patch_core_offsets, w_first, w_second, w_coarse, w_head):
    halo_count = lax.axis_size("halo")
    tile_count = lax.axis_size("blocks") * lax.axis_size("gz")
    vmem = pl.BlockSpec(memory_space=pltpu.VMEM)
    hbm = pl.BlockSpec(memory_space=HBM)

    ysides = [lax.ppermute(raw_volume, "halo", neighbour_pairs(halo_count, 0))]
    if halo_count > 2:
        ysides.append(lax.ppermute(raw_volume, "halo", neighbour_pairs(halo_count, 1)))

    first_taps = jnp.transpose(w_first, (1, 2, 3, 4, 0))
    held = [first_taps, w_coarse, w_head, raw_volume]
    sources = [first_taps, w_second, w_coarse, w_head, raw_volume]
    w2, first, coarse, head, raw = pl.pallas_call(
        prepare_second,
        out_shape=[jax.ShapeDtypeStruct((4096, 256), BF16)]
        + [jax.ShapeDtypeStruct(x.shape, BF16) for x in held],
        in_specs=[hbm] * 5,
        out_specs=[vmem] * 5,
        scratch_shapes=[
            pltpu.VMEM((27 * 64, 128), F32),
            pltpu.VMEM(w_second.shape, BF16),
            pltpu.SemaphoreType.DMA((5,)),
        ],
        compiler_params=pltpu.CompilerParams(vmem_limit_bytes=24 << 20),
        cost_estimate=pl.CostEstimate(flops=1 << 20, bytes_accessed=8 << 20, transcendentals=0),
    )(*(pltpu.with_memory_space_constraint(x, HBM) for x in sources))

    stack = jnp.stack([raw] + ysides)
    odd = lax.axis_index("gz") == 1
    first_layers, last_layers = stack[:, :MARGIN], stack[:, -MARGIN:]
    pair = lax.ppermute(jnp.where(odd, first_layers, last_layers), "gz", [(0, 1), (1, 0)])
    chain = lax.ppermute(
        jnp.where(odd, last_layers, first_layers),
        ("blocks", "halo", "gz"),
        chain_pairs(tile_count, halo_count),
    )

    w1, wc, wh = pl.pallas_call(
        prepare_rest,
        out_shape=[
            jax.ShapeDtypeStruct((256, 1792), BF16),
            jax.ShapeDtypeStruct((3456, 256), BF16),
            jax.ShapeDtypeStruct((240, 256), BF16),
        ],
        in_specs=[vmem] * 3,
        out_specs=[vmem] * 3,
        scratch_shapes=[pltpu.VMEM((27 * 64, 128), F32)],
        compiler_params=pltpu.CompilerParams(vmem_limit_bytes=16 << 20),
        cost_estimate=pl.CostEstimate(flops=1 << 20, bytes_accessed=6 << 20, transcendentals=0),
    )(first, coarse, head)

    def body(*refs):
        tile_kernel(halo_count, tile_count, *refs)

    return pl.pallas_call(
        body,
        out_shape=jax.ShapeDtypeStruct((3, 16, 8, 128), F32),
        in_specs=[hbm, hbm] + [vmem] * (7 + len(ysides)),
        out_specs=vmem,
        scratch_shapes=[
            pltpu.VMEM((2, 26, 16, 128), BF16),
            pltpu.VMEM((22, 80, 256), BF16),
            pltpu.VMEM((22, 2, 7, 64, 256), BF16),
            pltpu.VMEM((20, 4, 64, 256), BF16),
            pltpu.VMEM((20, 3, 64, 128), F32),
            pltpu.VMEM((MOST, 6, 64, 1152), BF16),
            pltpu.VMEM((16, 24, 128), F32),
            pltpu.VMEM((MOST, 4, 24, 128), F32),
            pltpu.VMEM((MOST, CORE, 3, 8, 128), F32),
            pltpu.SMEM(tissue_counts.shape, jnp.int32),
            pltpu.SMEM(patch_core_offsets.shape, jnp.int32),
            pltpu.SemaphoreType.DMA((2,)),
        ],
        compiler_params=pltpu.CompilerParams(vmem_limit_bytes=40 << 20),
        cost_estimate=pl.CostEstimate(flops=16 << 30, bytes_accessed=5 << 20, transcendentals=0),
    )(
        pltpu.with_memory_space_constraint(tissue_counts, HBM),
        pltpu.with_memory_space_constraint(patch_core_offsets, HBM),
        raw,
        *ysides,
        pair,
        chain,
        w1,
        w2,
        wc,
        wh,
    )


def solution(mesh):
    in_specs = (
        P(("groups", "blocks", "gz"), "halo", None),
        P(("groups", "blocks", "gz"), "halo", None),
        P(("groups", "blocks", "gz"), "halo", None),
        P(),
        P(),
        P(),
        P(),
    )
    out_specs = P(None, ("groups", "blocks", "gz"), "halo", None)
    return jax.shard_map(local, mesh=mesh, in_specs=in_specs, out_specs=out_specs, check_vma=False)
```
